32 devices in a mesh: space: 8 (over z, y), chan: 4 (over x, core).
Axes of the slice: x: 2, y: 2, z: 4, core: 2. Of those that a mesh axis runs over, the one named last changes fastest.
Arguments:
- features: bfloat16 [32, 128, 512], P('space', 'chan'), may hold values from -6 to 6
- occupancy: int32 [32, 512], P('space'), may hold values 0 or 1
- weight: bfloat16 [256, 27, 128], P('chan'), may hold values from -0.109375 to 0.109375
- cotangent: bfloat16 [32, 256, 512], P('space', 'chan'), may hold values from -6 to 6
- neighbours: int32 [32, 26], P('space'), may hold values from -1 to 31, as said below
Outputs:
- activation: bfloat16 [32, 256, 512], P('space', 'chan')
- input_grad: bfloat16 [32, 128, 512], P('space', 'chan')
- weight_grad: float32 [256, 27, 128], P('chan')
The draws below stay inside these ranges and needn't reach their ends.
Inputs may be any that keep to these rules, and one draw needn't show every extreme that they name: `neighbours`: each entry is -1 or a block id. With o = id // 4 the listing block's owner, an entry names a block of owner o, or, only for a listing block among the first 1 of its owner and only in columns 0 to 12, one of the last 1 block of owner o - 1, or, only for a listing block among the last 1 of its owner and only in columns 13 to 25, one of the first 1 block of owner o + 1. The same block may appear in several directions.
All inputs are finite; a program needn't handle non-finite values. No bound on the sum of `occupancy` on one device may be relied on, other than what follows from the above.
Results may differ from the reference program's by a relative error of at most 0.0049.
Values may be sent and summed in bfloat16 or wider, within the bound.
A program may use at most 64 MiB of HBM per device.

```python
import jax
import jax.numpy as jnp
from jax import lax

CIN = 128
COUT = 256
B_DEV = 4
BLOCKS = 32


def draw_neighbours(key, part):
    key = jax.random.fold_in(key, 11)
    first, second, third, fourth = jax.random.split(key, 4)
    rim_count = B_DEV // 4
    ids = jnp.arange(BLOCKS, dtype=jnp.int32)
    home = ids // B_DEV
    local_index = ids % B_DEV
    column = jnp.arange(26, dtype=jnp.int32)[None, :]
    lower_side = (local_index[:, None] < rim_count) & (column < 13)
    upper_side = (local_index[:, None] >= B_DEV - rim_count) & (column >= 13)
    boundary_passing = jax.random.randint(first, (BLOCKS, 26), 0, 2) == 1
    inside = home[:, None] * B_DEV + jax.random.randint(second, (BLOCKS, 26), 0, B_DEV)
    rim_pick = jax.random.randint(third, (BLOCKS, 26), 0, rim_count)
    below = (home[:, None] - 1) * B_DEV + B_DEV - 1 - rim_pick
    above = (home[:, None] + 1) * B_DEV + rim_pick
    result = jnp.where(lower_side & boundary_passing, below, jnp.where(upper_side & boundary_passing, above, inside))
    outside = (result < 0) | (result >= BLOCKS)
    empty = (jax.random.randint(fourth, (BLOCKS, 26), 0, 4) == 0) | outside
    result = jnp.where(empty, -1, result)
    result = result.at[0, 0].set(-1).at[BLOCKS - 1, 25].set(BLOCKS - 1)
    result = result.at[B_DEV, 0].set(B_DEV - 1).at[B_DEV - 1, 25].set(B_DEV)
    return result.astype(jnp.int32)


def with_ends(values, stream_key, smallest, top_value):
    longest = values.shape.index(max(values.shape))
    spots = []
    for shift in (0, 1):
        where = [jax.random.randint(jax.random.fold_in(stream_key, axis), (), 0, length) for axis, length in enumerate(values.shape)]
        where[longest] = (where[longest] + shift) % values.shape[longest]
        spots.append(tuple(where))
    return values.at[spots[0]].set(smallest).at[spots[1]].set(top_value)


def block_scale(rng, shape, cuts, low, high):
    level = 1.0
    for dim, shards_of in cuts:
        steps = jax.random.uniform(jax.random.fold_in(jax.random.fold_in(rng, 6), dim), (shards_of,), jnp.float32, low / len(cuts), high / len(cuts))
        level = level * jnp.repeat(jnp.exp(steps), shape[dim] // shards_of).reshape((-1,) + (1,) * (len(shape) - 1 - dim))
    return level


def scatter_about(key, extent, scale, limit, cuts=(), kind=jnp.bfloat16):
    drawn = jax.random.normal(key, extent, jnp.float32) * scale
    if len(cuts) > 0:
        drawn = block_scale(key, extent, cuts, -0.22, 0.18) * drawn
    return jnp.clip(drawn, min=-limit, max=limit).astype(kind)


def setup_inputs(seed: int = 0) -> dict:
    key_of = jax.random.split(jax.random.key(seed), 6)
    return {
        "features": scatter_about(key_of[0], (BLOCKS, CIN, 512), 1.0, 6.0, ((0, 8), (1, 4))),
        "occupancy": with_ends((jax.random.randint(key_of[1], (BLOCKS, 512), 0, 2) < 1).astype(jnp.int32), jax.random.fold_in(key_of[1], 1), 0, 1),
        "weight": scatter_about(key_of[2], (COUT, 27, CIN), (27 * CIN) ** -0.5, 0.109375, ((0, 4),)),
        "cotangent": scatter_about(key_of[3], (BLOCKS, COUT, 512), 1.0, 6.0, ((0, 8), (1, 4))),
        "neighbours": draw_neighbours(jax.random.fold_in(key_of[5], 71), 0),
    }


def offset_list():
    return [(a, b, c) for a in (-1, 0, 1) for b in (-1, 0, 1) for c in (-1, 0, 1)]

def span_pair(shift):
    if shift < 0:
        return ((0, 1), (7, 8))
    if shift == 0:
        return ((1, 9), (0, 8))
    return ((9, 10), (0, 1))

def cuts_for(a, b, c):
    spans = [span_pair(shift) for shift in (a, b, c)]
    padding_trimmed = (slice(None),) + tuple((slice(pair[0][0], pair[0][1]) for pair in spans))
    block_cut = (slice(None),) + tuple((slice(pair[1][0], pair[1][1]) for pair in spans))
    return (padding_trimmed, block_cut)

def assemble(blocks):
    channels = blocks.shape[1]
    cube_view = blocks.reshape(27, channels, 8, 8, 8)
    padded = jnp.zeros((channels, 10, 10, 10), blocks.dtype)
    for position, (a, b, c) in enumerate(offset_list()):
        padding_trimmed, block_cut = cuts_for(a, b, c)
        padded = padded.at[padding_trimmed].set(cube_view[position][block_cut])
    return padded

def cut_patch(padded, a, b, c):
    return padded[:, 1 + a:9 + a, 1 + b:9 + b, 1 + c:9 + c].reshape(padded.shape[0], 512)

def unpatch(grads):
    channels = grads[0].shape[0]
    padded_grad = jnp.zeros((channels, 10, 10, 10), jnp.float32)
    for position, (a, b, c) in enumerate(offset_list()):
        padded_grad = padded_grad.at[:, 1 + a:9 + a, 1 + b:9 + b, 1 + c:9 + c].add(grads[position].reshape(channels, 8, 8, 8))
    return padded_grad

def spread(padded_grad):
    channels = padded_grad.shape[0]
    pieces = []
    for a, b, c in offset_list():
        padding_trimmed, block_cut = cuts_for(a, b, c)
        piece_grid = jnp.zeros((channels, 8, 8, 8), jnp.float32).at[block_cut].set(padded_grad[padding_trimmed])
        pieces.append(piece_grid.reshape(channels, 512))
    return jnp.stack(pieces)

def reference(features, occupancy, weight, cotangent, neighbours):
    active_voxel_mask = occupancy.astype(jnp.bfloat16)
    mask_applied = features * active_voxel_mask[:, None, :]
    blocks_total = features.shape[0]
    self_ids = jnp.arange(blocks_total, dtype=jnp.int32)[:, None]
    every_index_list = jnp.concatenate([neighbours[:, :13], self_ids, neighbours[:, 13:]], axis=1).astype(jnp.int32)
    weight32 = weight.astype(jnp.float32)
    cout = weight.shape[0]
    cin = weight.shape[2]

    def visit(totals, position):
        weight_running_sum, grad_acc = totals
        row_ids = every_index_list[position]
        present = row_ids >= 0
        safe_ids = jnp.maximum(row_ids, 0)
        blocks = mask_applied[safe_ids] * present.astype(jnp.bfloat16)[:, None, None]
        padded = assemble(blocks)
        patches = jnp.stack([cut_patch(padded, a, b, c) for a, b, c in offset_list()]).astype(jnp.float32)
        pre_act = jnp.einsum('okc,kcv->ov', weight32, patches)
        live_row = occupancy[position].astype(jnp.float32)[None, :]
        output = (jax.nn.silu(pre_act) * live_row).astype(jnp.bfloat16)
        sigma = jax.nn.sigmoid(pre_act)
        slope = sigma * (1.0 + pre_act * (1.0 - sigma))
        grad_pre = (cotangent[position].astype(jnp.float32) * slope * live_row).astype(jnp.bfloat16)
        grad_pre32 = grad_pre.astype(jnp.float32)
        weight_running_sum = weight_running_sum + jnp.einsum('ov,kcv->okc', grad_pre32, patches)
        grad_patches = jnp.einsum('okc,ov->kcv', weight32, grad_pre32)
        pieces = spread(unpatch(grad_patches)) * present.astype(jnp.float32)[:, None, None]
        grad_acc = grad_acc.at[safe_ids].add(pieces)
        return ((weight_running_sum, grad_acc), output)
    start = (jnp.zeros((cout, 27, cin), jnp.float32), jnp.zeros((blocks_total, cin, 512), jnp.float32))
    (weight_running_sum, grad_acc), activation = lax.scan(visit, start, jnp.arange(blocks_total, dtype=jnp.int32))
    input_grad = (grad_acc * occupancy.astype(jnp.float32)[:, None, :]).astype(jnp.bfloat16)
    weight_grad = weight_running_sum * lax.rsqrt(jnp.float32(blocks_total * 512))
    return (activation, input_grad, weight_grad)
```

```python
import functools

import jax
import jax.numpy as jnp
from jax import lax
from jax.experimental import pallas as pl
from jax.experimental.pallas import tpu as pltpu
from jax.sharding import PartitionSpec as P

MESH = pl.DeviceIdType.MESH
F32 = jnp.float32
BF16 = jnp.bfloat16


def places(space_count):
    s, c = lax.axis_index("space"), lax.axis_index("chan")
    before = lax.rem(s + space_count - 1, space_count)
    after = lax.rem(s + 1, space_count)
    near = c + 1 - 2 * lax.rem(c, 2)
    far = lax.rem(c + 2, 4)
    return s, c, before, after, near, far


def greet(peers):
    barrier = pltpu.get_barrier_semaphore()
    for peer in peers:
        pl.semaphore_signal(barrier, inc=1, device_id=peer, device_id_type=MESH)
    pl.semaphore_wait(barrier, len(peers))


def gather_kernel(space_count, features_ref, occupancy_ref, full_ref, send_sem, recv_sem):
    blocks = features_ref.shape[0]
    s, c, before, after, near, far = places(space_count)

    def copy(slots, piece, to_slots, peer, index):
        return pltpu.make_async_remote_copy(
            src_ref=full_ref.at[slots, piece],
            dst_ref=full_ref.at[to_slots, piece],
            send_sem=send_sem.at[index],
            recv_sem=recv_sem.at[index],
            device_id=peer,
            device_id_type=MESH,
        )

    for b in range(blocks):
        mask = occupancy_ref[b : b + 1].astype(F32)
        full_ref[1 + b, c] = (features_ref[b].astype(F32) * mask).astype(BF16)
    greet([(before, c), (after, c), (s, near), (s, far)])
    own = pl.ds(1, blocks)
    low, high = 0, blocks + 1
    rim_down = copy(1, c, high, (before, c), 0)
    rim_up = copy(blocks, c, low, (after, c), 1)
    own_far = copy(own, c, own, (s, far), 2)
    own_near = copy(own, c, own, (s, near), 3)
    for each in (rim_down, rim_up, own_far, own_near):
        each.start()
    rim_down.wait_recv()
    rim_up.wait_recv()
    high_far = copy(high, c, high, (s, far), 4)
    low_far = copy(low, c, low, (s, far), 5)
    high_near = copy(high, c, high, (s, near), 6)
    low_near = copy(low, c, low, (s, near), 7)
    for each in (high_far, low_far, high_near, low_near):
        each.start()
    own_far.wait_recv()
    own_pass = copy(own, far, own, (s, near), 8)
    own_pass.start()
    high_far.wait_recv()
    low_far.wait_recv()
    high_pass = copy(high, far, high, (s, near), 9)
    low_pass = copy(low, far, low, (s, near), 10)
    high_pass.start()
    low_pass.start()
    for each in (own_near, high_near, low_near, own_pass, high_pass, low_pass):
        each.wait_recv()
    for each in (
        rim_down, rim_up, own_far, own_near, high_far, low_far,
        high_near, low_near, own_pass, high_pass, low_pass,
    ):
        each.wait_send()


def conv_kernel(
    neighbours_ref, full_ref, occupancy_ref, weight_ref, cotangent_ref,
    act_ref, grad_ref, wgrad_ref, cubes, sums, patches, grad_patches, wsum,
):
    blocks = cotangent_ref.shape[0]
    outs = cotangent_ref.shape[1]
    slots = blocks + 2
    place = lax.axis_index("space")
    for slot in range(slots):
        cubes[slot] = full_ref[slot].astype(F32).T.reshape(8, 8, 8, 128)
    cubes[slots] = jnp.zeros((8, 8, 8, 128), F32)
    sums[...] = jnp.zeros(sums.shape, F32)
    wsum[...] = jnp.zeros(wsum.shape, F32)
    k = lax.broadcasted_iota(jnp.int32, (10, 8, 128), 1)
    blank = jnp.zeros((1, 8, 128), F32)

    def visit(p, carry):
        slot = {}
        for number in range(27):
            a, b, c = number // 9 - 1, number // 3 % 3 - 1, number % 3 - 1
            if number == 13:
                slot[a, b, c] = p + 1
            else:
                named = neighbours_ref[p, number - (number > 13)]
                slot[a, b, c] = jnp.where(named < 0, slots, named - place * blocks + 1)

        def plane_of(row):
            a = -1 if row == 0 else (1 if row == 9 else 0)
            return a, (row - 1) % 8

        for row in range(10):
            a, i = plane_of(row)

            def line(c):
                return jnp.concatenate(
                    [cubes[slot[a, -1, c], i, 7:8], cubes[slot[a, 0, c], i], cubes[slot[a, 1, c], i, 0:1]],
                    axis=0,
                )

            middle = line(0)
            views = (
                pltpu.roll(jnp.where(k == 7, line(-1), middle), 1, 1),
                middle,
                pltpu.roll(jnp.where(k == 0, line(1), middle), 7, 1),
            )
            for b in range(3):
                for c in range(3):
                    piece = views[c][b : b + 8].reshape(64, 128).astype(BF16)
                    patches[64 * row : 64 * row + 64, (3 * b + c) * 128 : (3 * b + c + 1) * 128] = piece

        weight = weight_ref[...]
        product = lax.dot_general(
            weight, patches[...], (((1,), (1,)), ((), ())), preferred_element_type=F32
        )
        pre_act = (
            product[:outs, 0:512] + product[outs : 2 * outs, 64:576] + product[2 * outs :, 128:640]
        )
        live = occupancy_ref[p].astype(F32)
        sigma = jax.nn.sigmoid(pre_act)
        act_ref[p] = (pre_act * sigma * live).astype(BF16)
        slope = sigma * (1.0 + pre_act * (1.0 - sigma))
        grad_pre = (cotangent_ref[p].astype(F32) * slope * live).astype(BF16)
        half = jnp.zeros((outs, 64), BF16)
        wide = jnp.zeros((outs, 128), BF16)
        shifted = jnp.concatenate(
            [
                jnp.concatenate([grad_pre, wide], axis=1),
                jnp.concatenate([half, grad_pre, half], axis=1),
                jnp.concatenate([wide, grad_pre], axis=1),
            ],
            axis=0,
        )
        wsum[...] += jnp.dot(shifted, patches[...], preferred_element_type=F32)
        grad_patches[...] = lax.dot_general(
            shifted, weight, (((0,), (0,)), ((), ())), preferred_element_type=F32
        )

        for row in range(10):
            a, i = plane_of(row)

            def part(b, c):
                column = (3 * b + c) * 128
                return grad_patches[64 * row : 64 * row + 64, column : column + 128].reshape(8, 8, 128)

            def line_sum(c):
                return (
                    jnp.concatenate([part(0, c), blank, blank], axis=0)
                    + jnp.concatenate([blank, part(1, c), blank], axis=0)
                    + jnp.concatenate([blank, blank, part(2, c)], axis=0)
                )

            below = pltpu.roll(line_sum(0), 7, 1)
            above = pltpu.roll(line_sum(2), 1, 1)
            zero = jnp.zeros_like(below)
            middle = line_sum(1) + jnp.where(k == 7, zero, below) + jnp.where(k == 0, zero, above)
            for c, value in (
                (0, middle),
                (-1, jnp.where(k == 7, below, zero)),
                (1, jnp.where(k == 0, above, zero)),
            ):
                sums[slot[a, -1, c], i, 7:8] += value[0:1]
                sums[slot[a, 0, c], i] += value[1:9]
                sums[slot[a, 1, c], i, 0:1] += value[9:10]
        return carry

    lax.fori_loop(0, blocks, visit, 0)
    for slot in range(slots):
        grad_ref[slot] = sums[slot].reshape(512, 128).T.astype(BF16)
    rows = wsum.shape[0]
    for part in range(9):
        wgrad_ref[rows * part : rows * (part + 1)] = wsum[:, 128 * part : 128 * (part + 1)].astype(BF16)
    rest = wgrad_ref.shape[0] - 9 * rows
    if rest:
        wgrad_ref[9 * rows :] = jnp.zeros((rest, 128), BF16)


def reduce_kernel(
    space_count, with_weight, grad_ref, occupancy_ref, wgrad_ref, out_ref, wout_ref,
    near_buf, kept, passed, far_buf, rim_out, rim_in, wbuf,
    near_send, near_recv, far_send, far_recv, rim_send, rim_recv,
    scatter_send, scatter_recv, gather_send, gather_recv,
):
    blocks = out_ref.shape[0]
    s, c, before, after, near, far = places(space_count)
    peers = [lax.rem(s + d, space_count) for d in range(1, space_count)] if with_weight else [before, after]
    greet([(peer, c) for peer in peers] + [(s, near), (s, far)])

    def copy(source, target, send, recv, index, peer):
        return pltpu.make_async_remote_copy(
            src_ref=source,
            dst_ref=target,
            send_sem=send.at[index],
            recv_sem=recv.at[index],
            device_id=peer,
            device_id_type=MESH,
        )

    to_near = [
        copy(grad_ref.at[:, lax.rem(near, 2) + 2 * h], near_buf.at[h], near_send, near_recv, h, (s, near))
        for h in range(2)
    ]
    for each in to_near:
        each.start()
    scatters = []
    if with_weight:
        for d, peer in enumerate(peers):
            scatters.append(copy(wgrad_ref.at[peer], wbuf.at[d], scatter_send, scatter_recv, d, (peer, c)))
            scatters[-1].start()
    for each in to_near:
        each.wait_recv()
    mine, other = lax.div(c, 2), lax.div(far, 2)
    low, high = 0, blocks + 1
    own = pl.ds(1, blocks)
    to_far = [
        copy(passed.at[which], far_buf.at[which], far_send, far_recv, index, (s, far))
        for index, which in enumerate((low, high, own))
    ]
    for slots, sends in (((low, high), to_far[:2]), (range(1, blocks + 1), to_far[2:])):
        for slot in slots:
            passed[slot] = (grad_ref[slot, far].astype(F32) + near_buf[other, slot].astype(F32)).astype(BF16)
        for each in sends:
            each.start()
    for slot in range(blocks + 2):
        kept[slot] = grad_ref[slot, c].astype(F32) + near_buf[mine, slot].astype(F32)
    rims = []
    for index, (slot, peer) in enumerate(((low, before), (high, after))):
        to_far[index].wait_recv()
        rim_out[index] = (kept[slot] + far_buf[slot].astype(F32)).astype(BF16)
        rims.append(copy(rim_out.at[index], rim_in.at[index], rim_send, rim_recv, index, (peer, c)))
        rims[-1].start()
    to_far[2].wait_recv()
    for each in rims:
        each.wait_recv()
    for b in range(blocks):
        total = kept[1 + b] + far_buf[1 + b].astype(F32)
        if b == blocks - 1:
            total = total + rim_in[0].astype(F32)
        if b == 0:
            total = total + rim_in[1].astype(F32)
        out_ref[b] = (total * occupancy_ref[b : b + 1].astype(F32)).astype(BF16)
    if with_weight:
        total = wgrad_ref[s].astype(F32)
        for d, each in enumerate(scatters):
            each.wait_recv()
            total = total + wbuf[d].astype(F32)
        wout_ref[s] = total.astype(BF16)
        gathers = []
        for d, peer in enumerate(peers):
            gathers.append(copy(wout_ref.at[s], wout_ref.at[s], gather_send, gather_recv, d, (peer, c)))
            gathers[-1].start()
        for each in gathers:
            each.wait_recv()
        for each in scatters + gathers:
            each.wait_send()
    else:
        wout_ref[...] = wgrad_ref[...]
    for each in to_near + to_far + rims:
        each.wait_send()


def on_device(space_count, features, occupancy, weight, cotangent, neighbours):
    blocks, share = features.shape[:2]
    outs, _, cin = weight.shape
    slots = blocks + 2
    chans = cin // share
    with_weight = space_count <= 16
    vmem = pl.BlockSpec(memory_space=pltpu.VMEM)
    smem = pl.BlockSpec(memory_space=pltpu.SMEM)
    dma = pltpu.SemaphoreType.DMA

    full = pl.pallas_call(
        functools.partial(gather_kernel, space_count),
        out_shape=jax.ShapeDtypeStruct((slots, chans, share, 512), BF16),
        in_specs=[vmem] * 2,
        out_specs=vmem,
        scratch_shapes=[dma((11,)), dma((11,))],
        compiler_params=pltpu.CompilerParams(collective_id=0, has_side_effects=True),
        name="gather_blocks",
    )(features, occupancy)

    weight3 = jnp.transpose(weight.reshape(outs, 3, 9 * cin), (1, 0, 2)).reshape(3 * outs, 9 * cin)
    piece = -(-27 * outs // (16 * space_count)) * 16 if with_weight else 27 * outs // 4
    pieces = space_count if with_weight else 4
    act, grads, wgrad = pl.pallas_call(
        conv_kernel,
        out_shape=[
            jax.ShapeDtypeStruct(cotangent.shape, BF16),
            jax.ShapeDtypeStruct((slots, cin, 512), BF16),
            jax.ShapeDtypeStruct((pieces * piece, 128), BF16),
        ],
        in_specs=[smem] + [vmem] * 4,
        out_specs=[vmem] * 3,
        scratch_shapes=[
            pltpu.VMEM((slots + 1, 8, 8, 8, 128), F32),
            pltpu.VMEM((slots + 1, 8, 8, 8, 128), F32),
            pltpu.VMEM((640, 9 * cin), BF16),
            pltpu.VMEM((640, 9 * cin), F32),
            pltpu.VMEM((3 * outs, 9 * cin), F32),
        ],
        compiler_params=pltpu.CompilerParams(vmem_limit_bytes=48 * 2**20),
        name="conv_both_ways",
    )(
        neighbours,
        full.reshape(slots, cin, 512),
        occupancy.reshape(blocks, 1, 512),
        weight3,
        cotangent,
    )

    peers = pieces - 1
    grid = (slots, share, 512)
    input_grad, wtotal = pl.pallas_call(
        functools.partial(reduce_kernel, space_count, with_weight),
        out_shape=[
            jax.ShapeDtypeStruct((blocks, share, 512), BF16),
            jax.ShapeDtypeStruct((pieces, piece, 128), BF16),
        ],
        in_specs=[vmem] * 3,
        out_specs=[vmem] * 2,
        scratch_shapes=[
            pltpu.VMEM((2,) + grid, BF16),
            pltpu.VMEM(grid, F32),
            pltpu.VMEM(grid, BF16),
            pltpu.VMEM(grid, BF16),
            pltpu.VMEM((2, share, 512), BF16),
            pltpu.VMEM((2, share, 512), BF16),
            pltpu.VMEM((peers, piece, 128), BF16),
            dma((2,)), dma((2,)), dma((3,)), dma((3,)), dma((2,)), dma((2,)),
            dma((peers,)), dma((peers,)), dma((peers,)), dma((peers,)),
        ],
        compiler_params=pltpu.CompilerParams(
            collective_id=1, has_side_effects=True, vmem_limit_bytes=48 * 2**20
        ),
        name="reduce_grads",
    )(grads.reshape(slots, chans, share, 512), occupancy, wgrad.reshape(pieces, piece, 128))

    wflat = wtotal.reshape(pieces * piece, 128)[: 27 * outs].astype(F32)
    if not with_weight:
        wflat = lax.psum(wflat, "space")
    scaled = wflat * lax.rsqrt(F32(space_count * blocks * 512))
    weight_grad = jnp.transpose(scaled.reshape(9, 3, outs, cin), (2, 1, 0, 3)).reshape(outs, 27, cin)
    return (act, input_grad, weight_grad)


def solution(mesh):
    placed = (
        P("space", "chan", None),
        P("space", None),
        P("chan", None, None),
        P("space", "chan", None),
        P("space", None),
    )
    return jax.shard_map(
        functools.partial(on_device, mesh.shape["space"]),
        mesh=mesh,
        in_specs=placed,
        out_specs=(P("space", "chan", None), P("space", "chan", None), P("chan", None, None)),
        check_vma=False,
    )
```

```python
import functools

import jax
import jax.numpy as jnp
from jax import lax
from jax.experimental import pallas as pl
from jax.experimental.pallas import tpu as pltpu
from jax.sharding import PartitionSpec as P

MESH = pl.DeviceIdType.MESH
F32 = jnp.float32
BF16 = jnp.bfloat16


def places(space_count):
    s, c = lax.axis_index("space"), lax.axis_index("chan")
    before = lax.rem(s + space_count - 1, space_count)
    after = lax.rem(s + 1, space_count)
    near = c + 1 - 2 * lax.rem(c, 2)
    far = lax.rem(c + 2, 4)
    return s, c, before, after, near, far


def greet(peers):
    barrier = pltpu.get_barrier_semaphore()
    for peer in peers:
        pl.semaphore_signal(barrier, inc=1, device_id=peer, device_id_type=MESH)
    pl.semaphore_wait(barrier, len(peers))


def whole_kernel(
    space_count, with_weight,
    neighbours_ref, features_ref, occupancy_ref, weight_ref, cotangent_ref,
    act_ref, out_ref, wout_ref,
    full, cubes, sums, patches, grad_patches, shifted, wsum,
    wsend, ybuf, zsend, zbuf, wown, grads, near_buf, kept, passed, far_buf, rim_out, rim_in,
    load_send, load_recv, near_send, near_recv, far_send, far_recv, rim_send, rim_recv,
    y_send, y_recv, z_send, z_recv, zg_send, zg_recv, yg_send, yg_recv,
):
    blocks, share = features_ref.shape[:2]
    outs = cotangent_ref.shape[1]
    slots = blocks + 2
    s, c, before, after, near, far = places(space_count)
    y = lax.rem(s, 2)
    z = lax.div(s, 2)
    beside = s + 1 - 2 * y

    def copy(source, target, send, recv, index, peer):
        return pltpu.make_async_remote_copy(
            src_ref=source,
            dst_ref=target,
            send_sem=send.at[index],
            recv_sem=recv.at[index],
            device_id=peer,
            device_id_type=MESH,
        )

    peers = [(before, c), (after, c), (s, near), (s, far)]
    if with_weight:
        peers += [(lax.rem(s + 2 * d, space_count), c) for d in range(1, 4)]
    greet(peers)

    def spread(slots_from, piece, slots_to, peer, index):
        return copy(full.at[slots_from, piece], full.at[slots_to, piece], load_send, load_recv, index, peer)

    own = pl.ds(1, blocks)
    low, high = 0, blocks + 1
    for b in (0, blocks - 1, *range(1, blocks - 1)):
        mask = occupancy_ref[b : b + 1].astype(F32)
        full[1 + b, c] = (features_ref[b].astype(F32) * mask).astype(BF16)
    rim_down = spread(1, c, high, (before, c), 0)
    rim_up = spread(blocks, c, low, (after, c), 1)
    own_far = spread(own, c, own, (s, far), 2)
    own_near = spread(own, c, own, (s, near), 3)
    high_far = spread(high, c, high, (s, far), 4)
    low_far = spread(low, c, low, (s, far), 5)
    high_near = spread(high, c, high, (s, near), 6)
    low_near = spread(low, c, low, (s, near), 7)
    own_pass = spread(own, far, own, (s, near), 8)
    high_pass = spread(high, far, high, (s, near), 9)
    low_pass = spread(low, far, low, (s, near), 10)
    for each in (rim_down, rim_up, own_far, own_near):
        each.start()
    cubes[slots] = jnp.zeros((8, 8, 8, 128), F32)
    sums[...] = jnp.zeros(sums.shape, F32)
    wsum[...] = jnp.zeros(wsum.shape, F32)
    shifted[...] = jnp.zeros(shifted.shape, BF16)
    k = lax.broadcasted_iota(jnp.int32, (10, 8, 128), 1)
    blank = jnp.zeros((1, 8, 128), F32)
    own_far.wait_recv()
    own_pass.start()
    rim_down.wait_recv()
    rim_up.wait_recv()
    for each in (high_far, low_far, high_near, low_near):
        each.start()

    def turn(slot):
        cubes[slot] = full[slot].reshape(4 * share, 512).astype(F32).T.reshape(8, 8, 8, 128)

    own_near.wait_recv()
    own_pass.wait_recv()
    for slot in range(1, blocks + 1):
        turn(slot)

    def plane_of(row):
        a = -1 if row == 0 else (1 if row == 9 else 0)
        return a, (row - 1) % 8

    def offsets():
        for number in range(27):
            yield number, (number // 9 - 1, number // 3 % 3 - 1, number % 3 - 1)

    def forward(t, carry):
        p = lax.rem(t + 1, blocks)

        @pl.when(t == blocks - 2)
        def _():
            high_far.wait_recv()
            low_far.wait_recv()
            high_pass.start()
            low_pass.start()
            for each in (high_near, low_near, high_pass, low_pass):
                each.wait_recv()
            turn(low)
            turn(high)

        slot = {}
        for number, offset in offsets():
            if number == 13:
                slot[offset] = p + 1
            else:
                named = neighbours_ref[p, number - (number > 13)]
                near_id = jnp.clip(named - s * blocks + 1, 0, slots)
                slot[offset] = jnp.where(named < 0, slots, near_id)

        for row in range(10):
            a, i = plane_of(row)

            def line(c):
                return jnp.concatenate(
                    [cubes[slot[a, -1, c], i, 7:8], cubes[slot[a, 0, c], i], cubes[slot[a, 1, c], i, 0:1]],
                    axis=0,
                )

            middle = line(0)
            views = (
                pltpu.roll(jnp.where(k == 7, line(-1), middle), 1, 1),
                middle,
                pltpu.roll(jnp.where(k == 0, line(1), middle), 7, 1),
            )
            for b in range(3):
                for c in range(3):
                    piece = views[c][b : b + 8].reshape(64, 128).astype(BF16)
                    patches[64 * row : 64 * row + 64, (3 * b + c) * 128 : (3 * b + c + 1) * 128] = piece

        product = lax.dot_general(
            weight_ref[...], patches[...], (((1,), (1,)), ((), ())), preferred_element_type=F32
        )
        pre_act = (
            product[:outs, 0:512] + product[outs : 2 * outs, 64:576] + product[2 * outs :, 128:640]
        )
        live = occupancy_ref[pl.ds(p, 1)].astype(F32)
        sigma = jax.nn.sigmoid(pre_act)
        act_ref[p] = (pre_act * sigma * live).astype(BF16)
        slope = sigma * (1.0 + pre_act * (1.0 - sigma))
        grad_pre = (cotangent_ref[p].astype(F32) * slope * live).astype(BF16)
        half = jnp.zeros((outs, 64), BF16)
        shifted[p, :outs, 0:512] = grad_pre
        shifted[p, outs : 2 * outs] = jnp.concatenate([half, grad_pre, half], axis=1)
        shifted[p, 2 * outs :, 128:640] = grad_pre
        wsum[...] += jnp.dot(shifted[p], patches[...], preferred_element_type=F32)
        return carry

    lax.fori_loop(0, blocks, forward, 0)

    rows = wsum.shape[0]
    for part in range(9):
        wsend[rows * part : rows * (part + 1)] = wsum[:, 128 * part : 128 * (part + 1)].astype(BF16)
    rest = wsend.shape[0] - 9 * rows
    if rest:
        wsend[9 * rows :] = jnp.zeros((rest, 128), BF16)
    height = ybuf.shape[1]

    def cut(parity, place):
        return pl.ds(pl.multiple_of((parity * 4 + place) * height, 16), height)

    def to_beside(j):
        place = lax.rem(z + 1 + j, 4)
        return copy(wsend.at[cut(1 - y, place)], ybuf.at[place], y_send, y_recv, j, (beside, c))

    def to_level(j):
        place = lax.rem(z + 1 + j, 4)
        return copy(zsend.at[j], zbuf.at[j], z_send, z_recv, j, (2 * place + y, c))

    if with_weight:
        for j in range(4):
            to_beside(j).start()

    def backward(p, carry):
        grad_patches[...] = lax.dot_general(
            shifted[p], weight_ref[...], (((0,), (0,)), ((), ())), preferred_element_type=F32
        )
        share_of = {}
        for number, offset in offsets():
            if number == 13:
                named = s * blocks + p
            else:
                named = neighbours_ref[p, number - (number > 13)]
                named = jnp.where(named < 0, -9, named)
            for q in range(slots):
                share_of[q, offset] = jnp.where(named == s * blocks - 1 + q, 1.0, 0.0).astype(F32)

        for row in range(10):
            a, i = plane_of(row)

            def part(b, c):
                column = (3 * b + c) * 128
                return grad_patches[64 * row : 64 * row + 64, column : column + 128].reshape(8, 8, 128)

            def line_sum(c):
                return (
                    jnp.concatenate([part(0, c), blank, blank], axis=0)
                    + jnp.concatenate([blank, part(1, c), blank], axis=0)
                    + jnp.concatenate([blank, blank, part(2, c)], axis=0)
                )

            below = pltpu.roll(line_sum(0), 7, 1)
            above = pltpu.roll(line_sum(2), 1, 1)
            zero = jnp.zeros_like(below)
            middle = line_sum(1) + jnp.where(k == 7, zero, below) + jnp.where(k == 0, zero, above)
            values = (jnp.where(k == 7, below, zero), middle, jnp.where(k == 0, above, zero))
            for q in range(slots):

                def weighed(b, first, last):
                    return sum(share_of[q, (a, b, c - 1)] * values[c][first:last] for c in range(3))

                delta = weighed(0, 1, 9)
                delta = jnp.concatenate(
                    [delta[0:1] + weighed(1, 9, 10), delta[1:7], delta[7:8] + weighed(-1, 0, 1)], axis=0
                )
                sums[q, i] = sums[q, i] + delta

        if with_weight:
            to_beside(p).wait_recv()
            place = lax.rem(z + 1 + p, 4)
            joined = wsend[cut(y, place)].astype(F32) + ybuf[place].astype(F32)

            @pl.when(p < 3)
            def _():
                zsend[p] = joined.astype(BF16)
                to_level(p).start()

            @pl.when(p == 3)
            def _():
                wown[...] = joined

        return carry

    lax.fori_loop(0, blocks, backward, 0)

    for slot in range(slots):
        grads[slot] = sums[slot].reshape(512, 128).T.astype(BF16).reshape(4, share, 512)
    to_near = [
        copy(grads.at[:, lax.rem(near, 2) + 2 * h], near_buf.at[h], near_send, near_recv, h, (s, near))
        for h in range(2)
    ]
    for each in to_near:
        each.start()
    sent = [
        rim_down, rim_up, own_far, own_near, high_far, low_far,
        high_near, low_near, own_pass, high_pass, low_pass,
    ] + to_near
    if with_weight:
        total = wown[...]
        for j in range(3):
            to_level(j).wait_recv()
            total = total + zbuf[j].astype(F32)
        wout_ref[cut(y, z)] = total.astype(BF16)
        mine = wout_ref.at[cut(y, z)]
        levels = [
            copy(mine, mine, zg_send, zg_recv, j, (2 * lax.rem(z + 1 + j, 4) + y, c)) for j in range(3)
        ]
        asides = []
        for j in range(4):
            piece = wout_ref.at[cut(y, lax.rem(z + 4 - j, 4))]
            asides.append(copy(piece, piece, yg_send, yg_recv, j, (beside, c)))
        for each in levels + asides[:1]:
            each.start()
        sent += levels + asides + [to_beside(j) for j in range(4)] + [to_level(j) for j in range(3)]
    else:
        wout_ref[...] = wsend[...]

    for each in to_near:
        each.wait_recv()
    kin, other = lax.div(c, 2), lax.div(far, 2)
    to_far = [
        copy(passed.at[which], far_buf.at[which], far_send, far_recv, index, (s, far))
        for index, which in enumerate((low, high, own))
    ]
    for group, sends in (((low, high), to_far[:2]), (range(1, blocks + 1), to_far[2:])):
        for slot in group:
            passed[slot] = (grads[slot, far].astype(F32) + near_buf[other, slot].astype(F32)).astype(BF16)
        for each in sends:
            each.start()
    for slot in range(slots):
        kept[slot] = grads[slot, c].astype(F32) + near_buf[kin, slot].astype(F32)
    rims = []
    for index, (slot, peer) in enumerate(((low, before), (high, after))):
        to_far[index].wait_recv()
        rim_out[index] = (kept[slot] + far_buf[slot].astype(F32)).astype(BF16)
        rims.append(copy(rim_out.at[index], rim_in.at[index], rim_send, rim_recv, index, (peer, c)))
        rims[-1].start()
    sent += to_far + rims
    if with_weight:
        for j in range(3):
            levels[j].wait_recv()
            asides[j + 1].start()
    to_far[2].wait_recv()
    for each in rims:
        each.wait_recv()
    for b in range(blocks):
        total = kept[1 + b] + far_buf[1 + b].astype(F32)
        if b == blocks - 1:
            total = total + rim_in[0].astype(F32)
        if b == 0:
            total = total + rim_in[1].astype(F32)
        out_ref[b] = (total * occupancy_ref[b : b + 1].astype(F32)).astype(BF16)
    if with_weight:
        for each in asides:
            each.wait_recv()
    for each in sent:
        each.wait_send()


def on_device(space_count, features, occupancy, weight, cotangent, neighbours):
    blocks, share = features.shape[:2]
    outs, _, cin = weight.shape
    slots = blocks + 2
    with_weight = space_count == 8 and blocks == 4
    height = -(-27 * outs // 128) * 16
    vmem = pl.BlockSpec(memory_space=pltpu.VMEM)
    smem = pl.BlockSpec(memory_space=pltpu.SMEM)
    dma = pltpu.SemaphoreType.DMA
    weight3 = jnp.transpose(weight.reshape(outs, 3, 9 * cin), (1, 0, 2)).reshape(3 * outs, 9 * cin)
    grid = (slots, share, 512)
    act, input_grad, wtotal = pl.pallas_call(
        functools.partial(whole_kernel, space_count, with_weight),
        out_shape=[
            jax.ShapeDtypeStruct(cotangent.shape, BF16),
            jax.ShapeDtypeStruct((blocks, share, 512), BF16),
            jax.ShapeDtypeStruct((8 * height, 128), BF16),
        ],
        in_specs=[smem] + [vmem] * 4,
        out_specs=[vmem] * 3,
        scratch_shapes=[
            pltpu.VMEM((slots, 4, share, 512), BF16),
            pltpu.VMEM((slots + 1, 8, 8, 8, 128), F32),
            pltpu.VMEM((slots, 8, 8, 8, 128), F32),
            pltpu.VMEM((640, 9 * cin), BF16),
            pltpu.VMEM((640, 9 * cin), F32),
            pltpu.VMEM((blocks, 3 * outs, 640), BF16),
            pltpu.VMEM((3 * outs, 9 * cin), F32),
            pltpu.VMEM((8 * height, 128), BF16),
            pltpu.VMEM((4, height, 128), BF16),
            pltpu.VMEM((3, height, 128), BF16),
            pltpu.VMEM((3, height, 128), BF16),
            pltpu.VMEM((height, 128), F32),
            pltpu.VMEM((slots, 4, share, 512), BF16),
            pltpu.VMEM((2,) + grid, BF16),
            pltpu.VMEM(grid, F32),
            pltpu.VMEM(grid, BF16),
            pltpu.VMEM(grid, BF16),
            pltpu.VMEM((2, share, 512), BF16),
            pltpu.VMEM((2, share, 512), BF16),
        ]
        + [dma((n,)) for n in (11, 11, 2, 2, 3, 3, 2, 2, 4, 4, 3, 3, 3, 3, 4, 4)],
        compiler_params=pltpu.CompilerParams(
            collective_id=0, has_side_effects=True, vmem_limit_bytes=48 * 2**20
        ),
        name="conv_both_ways",
    )(neighbours, features, occupancy, weight3, cotangent)

    wflat = wtotal[: 27 * outs].astype(F32)
    if not with_weight:
        wflat = lax.psum(wflat, "space")
    scaled = wflat * lax.rsqrt(F32(space_count * blocks * 512))
    weight_grad = jnp.transpose(scaled.reshape(9, 3, outs, cin), (2, 1, 0, 3)).reshape(outs, 27, cin)
    return (act, input_grad, weight_grad)


def solution(mesh):
    placed = (
        P("space", "chan", None),
        P("space", None),
        P("chan", None, None),
        P("space", "chan", None),
        P("space", None),
    )
    return jax.shard_map(
        functools.partial(on_device, mesh.shape["space"]),
        mesh=mesh,
        in_specs=placed,
        out_specs=(P("space", "chan", None), P("space", "chan", None), P("chan", None, None)),
        check_vma=False,
    )
```

```python
import functools

import jax
import jax.numpy as jnp
from jax import lax
from jax.experimental import pallas as pl
from jax.experimental.pallas import tpu as pltpu
from jax.sharding import PartitionSpec as P

MESH = pl.DeviceIdType.MESH
F32 = jnp.float32
BF16 = jnp.bfloat16


def places(space_count):
    s, c = lax.axis_index("space"), lax.axis_index("chan")
    before = lax.rem(s + space_count - 1, space_count)
    after = lax.rem(s + 1, space_count)
    near = c + 1 - 2 * lax.rem(c, 2)
    far = lax.rem(c + 2, 4)
    return s, c, before, after, near, far


def greet(peers):
    barrier = pltpu.get_barrier_semaphore()
    for peer in peers:
        pl.semaphore_signal(barrier, inc=1, device_id=peer, device_id_type=MESH)
    pl.semaphore_wait(barrier, len(peers))


def whole_kernel(
    space_count, with_weight,
    neighbours_ref, features_ref, occupancy_ref, weight_hbm, cotangent_hbm,
    act_ref, out_ref, wout_ref,
    weight_ref, cotangent_ref, full, cubes, sums, patches, grad_patches, shifted, wsum,
    wsend, ybuf, zsend, zbuf, wown, grads, near_buf, kept, passed, far_buf, rim_out, rim_in,
    fetch, load_send, load_recv, near_send, near_recv, far_send, far_recv, rim_send, rim_recv,
    y_send, y_recv, z_send, z_recv, zg_send, zg_recv, yg_send, yg_recv,
):
    blocks, share = features_ref.shape[:2]
    outs = cotangent_ref.shape[1]
    slots = blocks + 2
    fetches = [pltpu.make_async_copy(cotangent_hbm, cotangent_ref, fetch.at[27])]
    for n in range(27):
        rows, columns = pl.ds(n // 9 * outs, outs), pl.ds(n % 9 * 128, 128)
        fetches.append(pltpu.make_async_copy(weight_hbm.at[n], weight_ref.at[rows, columns], fetch.at[n]))
    for each in fetches:
        each.start()
    s, c, before, after, near, far = places(space_count)
    y = lax.rem(s, 2)
    z = lax.div(s, 2)
    beside = s + 1 - 2 * y

    def copy(source, target, send, recv, index, peer):
        return pltpu.make_async_remote_copy(
            src_ref=source,
            dst_ref=target,
            send_sem=send.at[index],
            recv_sem=recv.at[index],
            device_id=peer,
            device_id_type=MESH,
        )

    peers = [(before, c), (after, c), (s, near), (s, far)]
    if with_weight:
        peers += [(lax.rem(s + 2 * d, space_count), c) for d in range(1, 4)]
    greet(peers)

    def spread(slots_from, piece, slots_to, peer, index):
        return copy(full.at[slots_from, piece], full.at[slots_to, piece], load_send, load_recv, index, peer)

    own = pl.ds(1, blocks)
    low, high = 0, blocks + 1
    for b in (0, blocks - 1, *range(1, blocks - 1)):
        mask = occupancy_ref[b : b + 1].astype(F32)
        full[1 + b, c] = (features_ref[b].astype(F32) * mask).astype(BF16)
    rim_down = spread(1, c, high, (before, c), 0)
    rim_up = spread(blocks, c, low, (after, c), 1)
    own_far = spread(own, c, own, (s, far), 2)
    own_near = spread(own, c, own, (s, near), 3)
    high_far = spread(high, c, high, (s, far), 4)
    low_far = spread(low, c, low, (s, far), 5)
    high_near = spread(high, c, high, (s, near), 6)
    low_near = spread(low, c, low, (s, near), 7)
    own_pass = spread(own, far, own, (s, near), 8)
    high_pass = spread(high, far, high, (s, near), 9)
    low_pass = spread(low, far, low, (s, near), 10)
    for each in (rim_down, rim_up, own_far, own_near):
        each.start()
    cubes[slots] = jnp.zeros((8, 8, 8, 128), F32)
    sums[...] = jnp.zeros(sums.shape, F32)
    wsum[...] = jnp.zeros(wsum.shape, F32)
    shifted[...] = jnp.zeros(shifted.shape, BF16)
    k = lax.broadcasted_iota(jnp.int32, (10, 8, 128), 1)
    blank = jnp.zeros((1, 8, 128), F32)
    own_far.wait_recv()
    own_pass.start()
    rim_down.wait_recv()
    rim_up.wait_recv()
    for each in (high_far, low_far, high_near, low_near):
        each.start()

    def turn(slot):
        cubes[slot] = full[slot].reshape(4 * share, 512).astype(F32).T.reshape(8, 8, 8, 128)

    for each in fetches:
        each.wait()
    own_near.wait_recv()
    own_pass.wait_recv()
    for slot in range(1, blocks + 1):
        turn(slot)

    def plane_of(row):
        a = -1 if row == 0 else (1 if row == 9 else 0)
        return a, (row - 1) % 8

    def offsets():
        for number in range(27):
            yield number, (number // 9 - 1, number // 3 % 3 - 1, number % 3 - 1)

    def forward(t, carry):
        p = lax.rem(t + 1, blocks)

        @pl.when(t == blocks - 2)
        def _():
            high_far.wait_recv()
            low_far.wait_recv()
            high_pass.start()
            low_pass.start()
            for each in (high_near, low_near, high_pass, low_pass):
                each.wait_recv()
            turn(low)
            turn(high)

        slot = {}
        for number, offset in offsets():
            if number == 13:
                slot[offset] = p + 1
            else:
                named = neighbours_ref[p, number - (number > 13)]
                near_id = jnp.clip(named - s * blocks + 1, 0, slots)
                slot[offset] = jnp.where(named < 0, slots, near_id)

        for row in range(10):
            a, i = plane_of(row)

            def line(c):
                return jnp.concatenate(
                    [cubes[slot[a, -1, c], i, 7:8], cubes[slot[a, 0, c], i], cubes[slot[a, 1, c], i, 0:1]],
                    axis=0,
                )

            middle = line(0)
            views = (
                pltpu.roll(jnp.where(k == 7, line(-1), middle), 1, 1),
                middle,
                pltpu.roll(jnp.where(k == 0, line(1), middle), 7, 1),
            )
            for b in range(3):
                for c in range(3):
                    piece = views[c][b : b + 8].reshape(64, 128).astype(BF16)
                    patches[64 * row : 64 * row + 64, (3 * b + c) * 128 : (3 * b + c + 1) * 128] = piece

        product = lax.dot_general(
            weight_ref[...], patches[...], (((1,), (1,)), ((), ())), preferred_element_type=F32
        )
        pre_act = (
            product[:outs, 0:512] + product[outs : 2 * outs, 64:576] + product[2 * outs :, 128:640]
        )
        live = occupancy_ref[pl.ds(p, 1)].astype(F32)
        sigma = jax.nn.sigmoid(pre_act)
        act_ref[p] = (pre_act * sigma * live).astype(BF16)
        slope = sigma * (1.0 + pre_act * (1.0 - sigma))
        grad_pre = (cotangent_ref[p].astype(F32) * slope * live).astype(BF16)
        half = jnp.zeros((outs, 64), BF16)
        shifted[p, :outs, 0:512] = grad_pre
        shifted[p, outs : 2 * outs] = jnp.concatenate([half, grad_pre, half], axis=1)
        shifted[p, 2 * outs :, 128:640] = grad_pre
        wsum[...] += jnp.dot(shifted[p], patches[...], preferred_element_type=F32)
        return carry

    lax.fori_loop(0, blocks, forward, 0)

    for n in range(27):
        part = wsum[n // 9 * outs : (n // 9 + 1) * outs, n % 9 * 128 : (n % 9 + 1) * 128]
        wsend[outs * n : outs * (n + 1)] = part.astype(BF16)
    rest = wsend.shape[0] - 27 * outs
    if rest:
        wsend[27 * outs :] = jnp.zeros((rest, 128), BF16)
    height = ybuf.shape[1]

    def cut(parity, place):
        return pl.ds(pl.multiple_of((parity * 4 + place) * height, 16), height)

    def to_beside(j):
        place = lax.rem(z + 1 + j, 4)
        return copy(wsend.at[cut(1 - y, place)], ybuf.at[place], y_send, y_recv, j, (beside, c))

    def to_level(j):
        place = lax.rem(z + 1 + j, 4)
        return copy(zsend.at[j], zbuf.at[j], z_send, z_recv, j, (2 * place + y, c))

    if with_weight:
        for j in range(4):
            to_beside(j).start()

    def targets(rim):
        return [*range(1, blocks + 1), *([] if rim is None else [rim])]

    def backward(p, j, rim):
        grad_patches[...] = lax.dot_general(
            shifted[p], weight_ref[...], (((0,), (0,)), ((), ())), preferred_element_type=F32
        )
        share_of = {}
        for number, offset in offsets():
            if number == 13:
                named = s * blocks + p
            else:
                named = neighbours_ref[p, number - (number > 13)]
                named = jnp.where(named < 0, -9, named)
            for index, q in enumerate(targets(rim)):
                share_of[index, offset] = jnp.where(named == s * blocks - 1 + q, 1.0, 0.0).astype(F32)

        for row in range(10):
            a, i = plane_of(row)

            def part(b, c):
                column = (3 * b + c) * 128
                return grad_patches[64 * row : 64 * row + 64, column : column + 128].reshape(8, 8, 128)

            def line_sum(c):
                return (
                    jnp.concatenate([part(0, c), blank, blank], axis=0)
                    + jnp.concatenate([blank, part(1, c), blank], axis=0)
                    + jnp.concatenate([blank, blank, part(2, c)], axis=0)
                )

            below = pltpu.roll(line_sum(0), 7, 1)
            above = pltpu.roll(line_sum(2), 1, 1)
            zero = jnp.zeros_like(below)
            middle = line_sum(1) + jnp.where(k == 7, zero, below) + jnp.where(k == 0, zero, above)
            values = (jnp.where(k == 7, below, zero), middle, jnp.where(k == 0, above, zero))
            for index, q in enumerate(targets(rim)):

                def weighed(b, first, last):
                    return sum(share_of[index, (a, b, c - 1)] * values[c][first:last] for c in range(3))

                delta = weighed(0, 1, 9)
                delta = jnp.concatenate(
                    [delta[0:1] + weighed(1, 9, 10), delta[1:7], delta[7:8] + weighed(-1, 0, 1)], axis=0
                )
                sums[q, i] = sums[q, i] + delta

        if with_weight:
            to_beside(j).wait_recv()
            place = lax.rem(z + 1 + j, 4)
            joined = wsend[cut(y, place)].astype(F32) + ybuf[place].astype(F32)

            @pl.when(j < 3)
            def _():
                zsend[j] = joined.astype(BF16)
                to_level(j).start()

            @pl.when(j == 3)
            def _():
                wown[...] = joined

    kin, other = lax.div(c, 2), lax.div(far, 2)
    parts = (low, high, own)
    to_near = [
        copy(
            grads.at[which, lax.rem(near, 2) + 2 * h], near_buf.at[h, which],
            near_send, near_recv, 2 * index + h, (s, near),
        )
        for index, which in enumerate(parts)
        for h in range(2)
    ]
    to_far = [
        copy(passed.at[which], far_buf.at[which], far_send, far_recv, index, (s, far))
        for index, which in enumerate(parts)
    ]
    rims = [
        copy(rim_out.at[index], rim_in.at[index], rim_send, rim_recv, index, (peer, c))
        for index, peer in enumerate((before, after))
    ]
    sent = [
        rim_down, rim_up, own_far, own_near, high_far, low_far,
        high_near, low_near, own_pass, high_pass, low_pass,
    ] + to_near + to_far + rims

    def flip(slot):
        grads[slot] = sums[slot].reshape(512, 128).T.astype(BF16).reshape(4, share, 512)

    def merge_near(slot):
        passed[slot] = (grads[slot, far].astype(F32) + near_buf[other, slot].astype(F32)).astype(BF16)
        kept[slot] = grads[slot, c].astype(F32) + near_buf[kin, slot].astype(F32)

    def edges(t, carry):
        backward(t * (blocks - 1), t, t * (blocks + 1))
        return carry

    def inner(p, carry):
        @pl.when(p == blocks - 2)
        def _():
            for each in to_near[:4]:
                each.wait_recv()
            for index, slot in enumerate((low, high)):
                merge_near(slot)
                to_far[index].start()

        backward(p, p + 1, None)
        return carry

    lax.fori_loop(0, 2, edges, 0)
    flip(low)
    flip(high)
    for each in to_near[:4]:
        each.start()
    lax.fori_loop(1, blocks - 1, inner, 0)

    for slot in range(1, blocks + 1):
        flip(slot)
    for each in to_near[4:]:
        each.start()
    if with_weight:
        total = wown[...]
        for j in range(3):
            to_level(j).wait_recv()
            total = total + zbuf[j].astype(F32)
        wout_ref[cut(y, z)] = total.astype(BF16)
        mine = wout_ref.at[cut(y, z)]
        levels = [
            copy(mine, mine, zg_send, zg_recv, j, (2 * lax.rem(z + 1 + j, 4) + y, c)) for j in range(3)
        ]
        asides = []
        for j in range(4):
            piece = wout_ref.at[cut(y, lax.rem(z + 4 - j, 4))]
            asides.append(copy(piece, piece, yg_send, yg_recv, j, (beside, c)))
        for each in levels + asides[:1]:
            each.start()
        sent += levels + asides + [to_beside(j) for j in range(4)] + [to_level(j) for j in range(3)]
    else:
        wout_ref[...] = wsend[...]

    for index, slot in enumerate((low, high)):
        to_far[index].wait_recv()
        rim_out[index] = (kept[slot] + far_buf[slot].astype(F32)).astype(BF16)
        rims[index].start()
    for each in to_near[4:]:
        each.wait_recv()
    for slot in range(1, blocks + 1):
        merge_near(slot)
    to_far[2].start()
    if with_weight:
        for j in range(3):
            levels[j].wait_recv()
            asides[j + 1].start()
    to_far[2].wait_recv()
    for each in rims:
        each.wait_recv()
    for b in range(blocks):
        total = kept[1 + b] + far_buf[1 + b].astype(F32)
        if b == blocks - 1:
            total = total + rim_in[0].astype(F32)
        if b == 0:
            total = total + rim_in[1].astype(F32)
        out_ref[b] = (total * occupancy_ref[b : b + 1].astype(F32)).astype(BF16)
    if with_weight:
        for each in asides:
            each.wait_recv()
    for each in sent:
        each.wait_send()


def on_device(space_count, features, occupancy, weight, cotangent, neighbours):
    blocks, share = features.shape[:2]
    outs, _, cin = weight.shape
    slots = blocks + 2
    with_weight = space_count == 8 and blocks == 4
    height = -(-27 * outs // 128) * 16
    vmem = pl.BlockSpec(memory_space=pltpu.VMEM)
    smem = pl.BlockSpec(memory_space=pltpu.SMEM)
    dma = pltpu.SemaphoreType.DMA
    grid = (slots, share, 512)
    act, input_grad, wtotal = pl.pallas_call(
        functools.partial(whole_kernel, space_count, with_weight),
        out_shape=[
            jax.ShapeDtypeStruct(cotangent.shape, BF16),
            jax.ShapeDtypeStruct((blocks, share, 512), BF16),
            jax.ShapeDtypeStruct((8 * height, 128), BF16),
        ],
        in_specs=[smem] + [vmem] * 2 + [pl.BlockSpec(memory_space=pl.ANY)] * 2,
        out_specs=[vmem] * 3,
        scratch_shapes=[
            pltpu.VMEM((3 * outs, 9 * cin), BF16),
            pltpu.VMEM(cotangent.shape, BF16),
            pltpu.VMEM((slots, 4, share, 512), BF16),
            pltpu.VMEM((slots + 1, 8, 8, 8, 128), F32),
            pltpu.VMEM((slots, 8, 8, 8, 128), F32),
            pltpu.VMEM((640, 9 * cin), BF16),
            pltpu.VMEM((640, 9 * cin), F32),
            pltpu.VMEM((blocks, 3 * outs, 640), BF16),
            pltpu.VMEM((3 * outs, 9 * cin), F32),
            pltpu.VMEM((8 * height, 128), BF16),
            pltpu.VMEM((4, height, 128), BF16),
            pltpu.VMEM((3, height, 128), BF16),
            pltpu.VMEM((3, height, 128), BF16),
            pltpu.VMEM((height, 128), F32),
            pltpu.VMEM((slots, 4, share, 512), BF16),
            pltpu.VMEM((2,) + grid, BF16),
            pltpu.VMEM(grid, F32),
            pltpu.VMEM(grid, BF16),
            pltpu.VMEM(grid, BF16),
            pltpu.VMEM((2, share, 512), BF16),
            pltpu.VMEM((2, share, 512), BF16),
        ]
        + [dma((n,)) for n in (28, 11, 11, 6, 6, 3, 3, 2, 2, 4, 4, 3, 3, 3, 3, 4, 4)],
        compiler_params=pltpu.CompilerParams(
            collective_id=0, has_side_effects=True, vmem_limit_bytes=48 * 2**20
        ),
        name="conv_both_ways",
    )(neighbours, features, occupancy, jnp.transpose(weight, (1, 0, 2)), cotangent)

    wflat = wtotal[: 27 * outs].astype(F32)
    if not with_weight:
        wflat = lax.psum(wflat, "space")
    scaled = wflat * lax.rsqrt(F32(space_count * blocks * 512))
    weight_grad = jnp.transpose(scaled.reshape(27, outs, cin), (1, 0, 2))
    return (act, input_grad, weight_grad)


def solution(mesh):
    placed = (
        P("space", "chan", None),
        P("space", None),
        P("chan", None, None),
        P("space", "chan", None),
        P("space", None),
    )
    return jax.shard_map(
        functools.partial(on_device, mesh.shape["space"]),
        mesh=mesh,
        in_specs=placed,
        out_specs=(P("space", "chan", None), P("space", "chan", None), P("chan", None, None)),
        check_vma=False,
    )
```

```python
import functools

import jax
import jax.numpy as jnp
from jax import lax
from jax.experimental import pallas as pl
from jax.experimental.pallas import tpu as pltpu
from jax.sharding import PartitionSpec as P

MESH = pl.DeviceIdType.MESH
F32 = jnp.float32
BF16 = jnp.bfloat16


def places(space_count):
    s, c = lax.axis_index("space"), lax.axis_index("chan")
    before = lax.rem(s + space_count - 1, space_count)
    after = lax.rem(s + 1, space_count)
    near = c + 1 - 2 * lax.rem(c, 2)
    far = lax.rem(c + 2, 4)
    return s, c, before, after, near, far


def greet(peers):
    barrier = pltpu.get_barrier_semaphore()
    for peer in peers:
        pl.semaphore_signal(barrier, inc=1, device_id=peer, device_id_type=MESH)
    return lambda: pl.semaphore_wait(barrier, len(peers))


def whole_kernel(
    space_count, with_weight,
    neighbours_hbm, features_hbm, occupancy_hbm, weight_hbm, cotangent_hbm,
    act_ref, out_ref, wout_ref,
    neighbours_ref, features_ref, occupancy_ref, weight_ref, cotangent_ref, full, cubes, sums, patches, grad_patches, shifted, wsum,
    wsend, ybuf, zsend, zbuf, wown, grads, near_buf, kept, passed, far_buf, rim_out, rim_in,
    fetch, load_send, load_recv, near_send, near_recv, far_send, far_recv, rim_send, rim_recv,
    y_send, y_recv, z_send, z_recv, zg_send, zg_recv, yg_send, yg_recv,
):
    blocks, share = features_ref.shape[:2]
    outs = cotangent_ref.shape[1]
    slots = blocks + 2
    first = [
        pltpu.make_async_copy(occupancy_hbm, occupancy_ref, fetch.at[28]),
        pltpu.make_async_copy(features_hbm, features_ref, fetch.at[29]),
    ]
    fetches = [
        pltpu.make_async_copy(neighbours_hbm, neighbours_ref, fetch.at[30]),
        pltpu.make_async_copy(cotangent_hbm, cotangent_ref, fetch.at[27]),
    ]
    for n in range(27):
        rows, columns = pl.ds(n // 9 * outs, outs), pl.ds(n % 9 * 128, 128)
        fetches.append(pltpu.make_async_copy(weight_hbm.at[n], weight_ref.at[rows, columns], fetch.at[n]))
    for each in first + fetches:
        each.start()
    s, c, before, after, near, far = places(space_count)
    y = lax.rem(s, 2)
    z = lax.div(s, 2)
    beside = s + 1 - 2 * y

    def copy(source, target, send, recv, index, peer):
        return pltpu.make_async_remote_copy(
            src_ref=source,
            dst_ref=target,
            send_sem=send.at[index],
            recv_sem=recv.at[index],
            device_id=peer,
            device_id_type=MESH,
        )

    peers = [(before, c), (after, c), (s, near), (s, far)]
    if with_weight:
        peers += [(lax.rem(s + 2 * d, space_count), c) for d in range(1, 4)]
    greeted = greet(peers)

    def spread(slots_from, piece, slots_to, peer, index):
        return copy(full.at[slots_from, piece], full.at[slots_to, piece], load_send, load_recv, index, peer)

    own = pl.ds(1, blocks)
    low, high = 0, blocks + 1
    for each in first:
        each.wait()
    for b in (0, blocks - 1, *range(1, blocks - 1)):
        mask = occupancy_ref[b : b + 1].astype(F32)
        full[1 + b, c] = (features_ref[b].astype(F32) * mask).astype(BF16)
    rim_down = spread(1, c, high, (before, c), 0)
    rim_up = spread(blocks, c, low, (after, c), 1)
    own_far = spread(own, c, own, (s, far), 2)
    own_near = spread(own, c, own, (s, near), 3)
    high_far = spread(high, c, high, (s, far), 4)
    low_far = spread(low, c, low, (s, far), 5)
    high_near = spread(high, c, high, (s, near), 6)
    low_near = spread(low, c, low, (s, near), 7)
    own_pass = spread(own, far, own, (s, near), 8)
    high_pass = spread(high, far, high, (s, near), 9)
    low_pass = spread(low, far, low, (s, near), 10)
    greeted()
    for each in (rim_down, rim_up, own_far, own_near):
        each.start()
    cubes[slots] = jnp.zeros((8, 8, 8, 128), F32)
    sums[...] = jnp.zeros(sums.shape, F32)
    wsum[...] = jnp.zeros(wsum.shape, F32)
    shifted[...] = jnp.zeros(shifted.shape, BF16)
    k = lax.broadcasted_iota(jnp.int32, (10, 8, 128), 1)
    blank = jnp.zeros((1, 8, 128), F32)
    own_far.wait_recv()
    own_pass.start()
    rim_down.wait_recv()
    rim_up.wait_recv()
    for each in (high_far, low_far, high_near, low_near):
        each.start()

    def turn(slot):
        cubes[slot] = full[slot].reshape(4 * share, 512).astype(F32).T.reshape(8, 8, 8, 128)

    for each in fetches:
        each.wait()
    own_near.wait_recv()
    own_pass.wait_recv()
    for slot in range(1, blocks + 1):
        turn(slot)

    def plane_of(row):
        a = -1 if row == 0 else (1 if row == 9 else 0)
        return a, (row - 1) % 8

    def offsets():
        for number in range(27):
            yield number, (number // 9 - 1, number // 3 % 3 - 1, number % 3 - 1)

    def forward(t, carry):
        p = lax.rem(t + 1, blocks)

        @pl.when(t == blocks - 2)
        def _():
            high_far.wait_recv()
            low_far.wait_recv()
            high_pass.start()
            low_pass.start()
            for each in (high_near, low_near, high_pass, low_pass):
                each.wait_recv()
            turn(low)
            turn(high)

        slot = {}
        for number, offset in offsets():
            if number == 13:
                slot[offset] = p + 1
            else:
                named = neighbours_ref[p, number - (number > 13)]
                near_id = jnp.clip(named - s * blocks + 1, 0, slots)
                slot[offset] = jnp.where(named < 0, slots, near_id)

        for row in range(10):
            a, i = plane_of(row)

            def line(c):
                return jnp.concatenate(
                    [cubes[slot[a, -1, c], i, 7:8], cubes[slot[a, 0, c], i], cubes[slot[a, 1, c], i, 0:1]],
                    axis=0,
                )

            middle = line(0)
            views = (
                pltpu.roll(jnp.where(k == 7, line(-1), middle), 1, 1),
                middle,
                pltpu.roll(jnp.where(k == 0, line(1), middle), 7, 1),
            )
            for b in range(3):
                for c in range(3):
                    piece = views[c][b : b + 8].reshape(64, 128).astype(BF16)
                    patches[64 * row : 64 * row + 64, (3 * b + c) * 128 : (3 * b + c + 1) * 128] = piece

        product = lax.dot_general(
            weight_ref[...], patches[...], (((1,), (1,)), ((), ())), preferred_element_type=F32
        )
        pre_act = (
            product[:outs, 0:512] + product[outs : 2 * outs, 64:576] + product[2 * outs :, 128:640]
        )
        live = occupancy_ref[pl.ds(p, 1)].astype(F32)
        sigma = jax.nn.sigmoid(pre_act)
        act_ref[p] = (pre_act * sigma * live).astype(BF16)
        slope = sigma * (1.0 + pre_act * (1.0 - sigma))
        grad_pre = (cotangent_ref[p].astype(F32) * slope * live).astype(BF16)
        half = jnp.zeros((outs, 64), BF16)
        shifted[p, :outs, 0:512] = grad_pre
        shifted[p, outs : 2 * outs] = jnp.concatenate([half, grad_pre, half], axis=1)
        shifted[p, 2 * outs :, 128:640] = grad_pre
        wsum[...] += jnp.dot(shifted[p], patches[...], preferred_element_type=F32)
        return carry

    lax.fori_loop(0, blocks, forward, 0)

    for n in range(27):
        part = wsum[n // 9 * outs : (n // 9 + 1) * outs, n % 9 * 128 : (n % 9 + 1) * 128]
        wsend[outs * n : outs * (n + 1)] = part.astype(BF16)
    rest = wsend.shape[0] - 27 * outs
    if rest:
        wsend[27 * outs :] = jnp.zeros((rest, 128), BF16)
    height = ybuf.shape[1]

    def cut(parity, place):
        return pl.ds(pl.multiple_of((parity * 4 + place) * height, 16), height)

    def to_beside(j):
        place = lax.rem(z + 1 + j, 4)
        return copy(wsend.at[cut(1 - y, place)], ybuf.at[place], y_send, y_recv, j, (beside, c))

    def to_level(j):
        place = lax.rem(z + 1 + j, 4)
        return copy(zsend.at[j], zbuf.at[j], z_send, z_recv, j, (2 * place + y, c))

    if with_weight:
        for j in range(4):
            to_beside(j).start()

    def targets(rim):
        return [*range(1, blocks + 1), *([] if rim is None else [rim])]

    def backward(p, j, rim):
        grad_patches[...] = lax.dot_general(
            shifted[p], weight_ref[...], (((0,), (0,)), ((), ())), preferred_element_type=F32
        )
        share_of = {}
        for number, offset in offsets():
            if number == 13:
                named = s * blocks + p
            else:
                named = neighbours_ref[p, number - (number > 13)]
                named = jnp.where(named < 0, -9, named)
            for index, q in enumerate(targets(rim)):
                share_of[index, offset] = jnp.where(named == s * blocks - 1 + q, 1.0, 0.0).astype(F32)

        for row in range(10):
            a, i = plane_of(row)

            def part(b, c):
                column = (3 * b + c) * 128
                return grad_patches[64 * row : 64 * row + 64, column : column + 128].reshape(8, 8, 128)

            def line_sum(c):
                return (
                    jnp.concatenate([part(0, c), blank, blank], axis=0)
                    + jnp.concatenate([blank, part(1, c), blank], axis=0)
                    + jnp.concatenate([blank, blank, part(2, c)], axis=0)
                )

            below = pltpu.roll(line_sum(0), 7, 1)
            above = pltpu.roll(line_sum(2), 1, 1)
            zero = jnp.zeros_like(below)
            middle = line_sum(1) + jnp.where(k == 7, zero, below) + jnp.where(k == 0, zero, above)
            values = (jnp.where(k == 7, below, zero), middle, jnp.where(k == 0, above, zero))
            for index, q in enumerate(targets(rim)):

                def weighed(b, first, last):
                    return sum(share_of[index, (a, b, c - 1)] * values[c][first:last] for c in range(3))

                delta = weighed(0, 1, 9)
                delta = jnp.concatenate(
                    [delta[0:1] + weighed(1, 9, 10), delta[1:7], delta[7:8] + weighed(-1, 0, 1)], axis=0
                )
                sums[q, i] = sums[q, i] + delta

        if with_weight:
            to_beside(j).wait_recv()
            place = lax.rem(z + 1 + j, 4)
            joined = wsend[cut(y, place)].astype(F32) + ybuf[place].astype(F32)

            @pl.when(j < 3)
            def _():
                zsend[j] = joined.astype(BF16)
                to_level(j).start()

            @pl.when(j == 3)
            def _():
                wown[...] = joined

    kin, other = lax.div(c, 2), lax.div(far, 2)
    parts = (low, high, own)
    to_near = [
        copy(
            grads.at[which, lax.rem(near, 2) + 2 * h], near_buf.at[h, which],
            near_send, near_recv, 2 * index + h, (s, near),
        )
        for index, which in enumerate(parts)
        for h in range(2)
    ]
    to_far = [
        copy(passed.at[which], far_buf.at[which], far_send, far_recv, index, (s, far))
        for index, which in enumerate(parts)
    ]
    rims = [
        copy(rim_out.at[index], rim_in.at[index], rim_send, rim_recv, index, (peer, c))
        for index, peer in enumerate((before, after))
    ]
    sent = [
        rim_down, rim_up, own_far, own_near, high_far, low_far,
        high_near, low_near, own_pass, high_pass, low_pass,
    ] + to_near + to_far + rims

    def flip(slot):
        grads[slot] = sums[slot].reshape(512, 128).T.astype(BF16).reshape(4, share, 512)

    def merge_near(slot):
        passed[slot] = (grads[slot, far].astype(F32) + near_buf[other, slot].astype(F32)).astype(BF16)
        kept[slot] = grads[slot, c].astype(F32) + near_buf[kin, slot].astype(F32)

    def edges(t, carry):
        backward(t * (blocks - 1), t, t * (blocks + 1))
        return carry

    def inner(p, carry):
        @pl.when(p == blocks - 2)
        def _():
            for each in to_near[:4]:
                each.wait_recv()
            for index, slot in enumerate((low, high)):
                merge_near(slot)
                to_far[index].start()

        backward(p, p + 1, None)
        return carry

    lax.fori_loop(0, 2, edges, 0)
    flip(low)
    flip(high)
    for each in to_near[:4]:
        each.start()
    lax.fori_loop(1, blocks - 1, inner, 0)

    for slot in range(1, blocks + 1):
        flip(slot)
    for each in to_near[4:]:
        each.start()
    if with_weight:
        total = wown[...]
        for j in range(3):
            to_level(j).wait_recv()
            total = total + zbuf[j].astype(F32)
        wout_ref[cut(y, z)] = total.astype(BF16)
        mine = wout_ref.at[cut(y, z)]
        levels = [
            copy(mine, mine, zg_send, zg_recv, j, (2 * lax.rem(z + 1 + j, 4) + y, c)) for j in range(3)
        ]
        asides = []
        for j in range(4):
            piece = wout_ref.at[cut(y, lax.rem(z + 4 - j, 4))]
            asides.append(copy(piece, piece, yg_send, yg_recv, j, (beside, c)))
        for each in levels + asides[:1]:
            each.start()
        sent += levels + asides + [to_beside(j) for j in range(4)] + [to_level(j) for j in range(3)]
    else:
        wout_ref[...] = wsend[...]

    for index, slot in enumerate((low, high)):
        to_far[index].wait_recv()
        rim_out[index] = (kept[slot] + far_buf[slot].astype(F32)).astype(BF16)
        rims[index].start()
    for each in to_near[4:]:
        each.wait_recv()
    for slot in range(1, blocks + 1):
        merge_near(slot)
    to_far[2].start()
    if with_weight:
        for j in range(3):
            levels[j].wait_recv()
            asides[j + 1].start()
    to_far[2].wait_recv()
    for each in rims:
        each.wait_recv()
    for b in range(blocks):
        total = kept[1 + b] + far_buf[1 + b].astype(F32)
        if b == blocks - 1:
            total = total + rim_in[0].astype(F32)
        if b == 0:
            total = total + rim_in[1].astype(F32)
        out_ref[b] = (total * occupancy_ref[b : b + 1].astype(F32)).astype(BF16)
    if with_weight:
        for each in asides:
            each.wait_recv()
    for each in sent:
        each.wait_send()


def finish_kernel(scale, act_ref, grad_ref, wgrad_ref, act_out, grad_out, wgrad_out):
    act_out[...] = act_ref[...]
    grad_out[...] = grad_ref[...]
    outs = wgrad_out.shape[1]
    for n in range(27):
        wgrad_out[n] = wgrad_ref[outs * n : outs * (n + 1)].astype(F32) * scale


def on_device(space_count, features, occupancy, weight, cotangent, neighbours):
    blocks, share = features.shape[:2]
    outs, _, cin = weight.shape
    slots = blocks + 2
    with_weight = space_count == 8 and blocks == 4
    height = -(-27 * outs // 128) * 16
    vmem = pl.BlockSpec(memory_space=pltpu.VMEM)
    dma = pltpu.SemaphoreType.DMA
    grid = (slots, share, 512)
    act, input_grad, wtotal = pl.pallas_call(
        functools.partial(whole_kernel, space_count, with_weight),
        out_shape=[
            jax.ShapeDtypeStruct(cotangent.shape, BF16),
            jax.ShapeDtypeStruct((blocks, share, 512), BF16),
            jax.ShapeDtypeStruct((8 * height, 128), BF16),
        ],
        in_specs=[pl.BlockSpec(memory_space=pltpu.HBM)] * 5,
        out_specs=[vmem] * 3,
        scratch_shapes=[
            pltpu.SMEM(neighbours.shape, jnp.int32),
            pltpu.VMEM(features.shape, BF16),
            pltpu.VMEM(occupancy.shape, jnp.int32),
            pltpu.VMEM((3 * outs, 9 * cin), BF16),
            pltpu.VMEM(cotangent.shape, BF16),
            pltpu.VMEM((slots, 4, share, 512), BF16),
            pltpu.VMEM((slots + 1, 8, 8, 8, 128), F32),
            pltpu.VMEM((slots, 8, 8, 8, 128), F32),
            pltpu.VMEM((640, 9 * cin), BF16),
            pltpu.VMEM((640, 9 * cin), F32),
            pltpu.VMEM((blocks, 3 * outs, 640), BF16),
            pltpu.VMEM((3 * outs, 9 * cin), F32),
            pltpu.VMEM((8 * height, 128), BF16),
            pltpu.VMEM((4, height, 128), BF16),
            pltpu.VMEM((3, height, 128), BF16),
            pltpu.VMEM((3, height, 128), BF16),
            pltpu.VMEM((height, 128), F32),
            pltpu.VMEM((slots, 4, share, 512), BF16),
            pltpu.VMEM((2,) + grid, BF16),
            pltpu.VMEM(grid, F32),
            pltpu.VMEM(grid, BF16),
            pltpu.VMEM(grid, BF16),
            pltpu.VMEM((2, share, 512), BF16),
            pltpu.VMEM((2, share, 512), BF16),
        ]
        + [dma((n,)) for n in (31, 11, 11, 6, 6, 3, 3, 2, 2, 4, 4, 3, 3, 3, 3, 4, 4)],
        compiler_params=pltpu.CompilerParams(
            collective_id=0, has_side_effects=True, vmem_limit_bytes=63 * 2**20
        ),
        name="conv_both_ways",
    )(neighbours, features, occupancy, jnp.transpose(weight, (1, 0, 2)), cotangent)

    if not with_weight:
        wtotal = lax.psum(wtotal.astype(F32), "space")
    act, input_grad, weight_grad = pl.pallas_call(
        functools.partial(finish_kernel, (space_count * blocks * 512) ** -0.5),
        out_shape=[
            jax.ShapeDtypeStruct(act.shape, BF16),
            jax.ShapeDtypeStruct(input_grad.shape, BF16),
            jax.ShapeDtypeStruct((27, outs, cin), F32),
        ],
        in_specs=[vmem] * 3,
        out_specs=[vmem] * 3,
        compiler_params=pltpu.CompilerParams(vmem_limit_bytes=63 * 2**20),
        name="finish",
    )(act, input_grad, wtotal)
    return (act, input_grad, jnp.transpose(weight_grad, (1, 0, 2)))


def solution(mesh):
    placed = (
        P("space", "chan", None),
        P("space", None),
        P("chan", None, None),
        P("space", "chan", None),
        P("space", None),
    )
    return jax.shard_map(
        functools.partial(on_device, mesh.shape["space"]),
        mesh=mesh,
        in_specs=placed,
        out_specs=(P("space", "chan", None), P("space", "chan", None), P("chan", None, None)),
        check_vma=False,
    )
```

```python
import functools

import jax
import jax.numpy as jnp
from jax import lax
from jax.experimental import pallas as pl
from jax.experimental.pallas import tpu as pltpu
from jax.sharding import PartitionSpec as P

MESH = pl.DeviceIdType.MESH
F32 = jnp.float32
BF16 = jnp.bfloat16


def places(space_count):
    s, c = lax.axis_index("space"), lax.axis_index("chan")
    before = lax.rem(s + space_count - 1, space_count)
    after = lax.rem(s + 1, space_count)
    near = c + 1 - 2 * lax.rem(c, 2)
    far = lax.rem(c + 2, 4)
    return s, c, before, after, near, far


def greet(peers):
    barrier = pltpu.get_barrier_semaphore()
    for peer in peers:
        pl.semaphore_signal(barrier, inc=1, device_id=peer, device_id_type=MESH)
    return lambda: pl.semaphore_wait(barrier, len(peers))


def whole_kernel(
    space_count, with_weight,
    neighbours_hbm, features_hbm, occupancy_hbm, weight_hbm, cotangent_hbm,
    act_ref, out_ref, wout_ref,
    neighbours_ref, features_ref, occupancy_ref, weight_ref, cotangent_ref, full, cubes, sums, patches, grad_patches, shifted, wsum,
    wsend, ybuf, zsend, zbuf, wown, grads, near_buf, kept, passed, far_buf, rim_out, rim_in,
    fetch, load_send, load_recv, near_send, near_recv, far_send, far_recv, rim_send, rim_recv,
    y_send, y_recv, z_send, z_recv, zg_send, zg_recv, yg_send, yg_recv,
):
    blocks, share = features_ref.shape[:2]
    outs = cotangent_ref.shape[1]
    slots = blocks + 2
    first = [
        pltpu.make_async_copy(occupancy_hbm, occupancy_ref, fetch.at[28]),
        pltpu.make_async_copy(features_hbm, features_ref, fetch.at[29]),
    ]
    fetches = [
        pltpu.make_async_copy(neighbours_hbm, neighbours_ref, fetch.at[30]),
        pltpu.make_async_copy(cotangent_hbm, cotangent_ref, fetch.at[27]),
    ]
    for n in range(27):
        rows, columns = pl.ds(n // 9 * outs, outs), pl.ds(n % 9 * 128, 128)
        fetches.append(pltpu.make_async_copy(weight_hbm.at[n], weight_ref.at[rows, columns], fetch.at[n]))
    for each in first + fetches:
        each.start()
    s, c, before, after, near, far = places(space_count)
    y = lax.rem(s, 2)
    z = lax.div(s, 2)
    beside = s + 1 - 2 * y

    def copy(source, target, send, recv, index, peer):
        return pltpu.make_async_remote_copy(
            src_ref=source,
            dst_ref=target,
            send_sem=send.at[index],
            recv_sem=recv.at[index],
            device_id=peer,
            device_id_type=MESH,
        )

    peers = [(before, c), (after, c), (s, near), (s, far)]
    if with_weight:
        peers += [(lax.rem(s + 2 * d, space_count), c) for d in range(1, 4)]
    greeted = greet(peers)

    def spread(slots_from, piece, slots_to, peer, index):
        return copy(full.at[slots_from, piece], full.at[slots_to, piece], load_send, load_recv, index, peer)

    own = pl.ds(1, blocks)
    low, high = 0, blocks + 1
    for each in first:
        each.wait()
    for b in (0, blocks - 1, *range(1, blocks - 1)):
        mask = occupancy_ref[b : b + 1].astype(F32)
        full[1 + b, c] = (features_ref[b].astype(F32) * mask).astype(BF16)
    rim_down = spread(1, c, high, (before, c), 0)
    rim_up = spread(blocks, c, low, (after, c), 1)
    own_near = spread(own, c, own, (s, near), 2)
    high_far = spread(high, c, high, (s, far), 3)
    low_far = spread(low, c, low, (s, far), 4)
    high_near = spread(high, c, high, (s, near), 5)
    low_near = spread(low, c, low, (s, near), 6)
    high_pass = spread(high, far, high, (s, near), 7)
    low_pass = spread(low, far, low, (s, near), 8)
    own_far = [spread(1 + b, c, 1 + b, (s, far), 9 + b) for b in range(blocks)]
    own_pass = [spread(1 + b, far, 1 + b, (s, near), 9 + blocks + b) for b in range(blocks)]
    greeted()
    for each in (rim_down, rim_up, *own_far, own_near):
        each.start()
    cubes[slots] = jnp.zeros((8, 8, 8, 128), F32)
    sums[...] = jnp.zeros(sums.shape, F32)
    wsum[...] = jnp.zeros(wsum.shape, F32)
    shifted[...] = jnp.zeros(shifted.shape, BF16)
    k = lax.broadcasted_iota(jnp.int32, (10, 8, 128), 1)
    blank = jnp.zeros((1, 8, 128), F32)
    for b in range(blocks):
        own_far[b].wait_recv()
        own_pass[b].start()
    rim_down.wait_recv()
    rim_up.wait_recv()
    for each in (high_far, low_far, high_near, low_near):
        each.start()

    def turn(slot):
        cubes[slot] = full[slot].reshape(4 * share, 512).astype(F32).T.reshape(8, 8, 8, 128)

    for each in fetches:
        each.wait()
    own_near.wait_recv()
    for b in range(blocks):
        own_pass[b].wait_recv()
        turn(1 + b)

    def plane_of(row):
        a = -1 if row == 0 else (1 if row == 9 else 0)
        return a, (row - 1) % 8

    def offsets():
        for number in range(27):
            yield number, (number // 9 - 1, number // 3 % 3 - 1, number % 3 - 1)

    def forward(t, carry):
        p = lax.rem(t + 1, blocks)

        @pl.when(t == blocks - 2)
        def _():
            high_far.wait_recv()
            low_far.wait_recv()
            high_pass.start()
            low_pass.start()
            for each in (high_near, low_near, high_pass, low_pass):
                each.wait_recv()
            turn(low)
            turn(high)

        slot = {}
        for number, offset in offsets():
            if number == 13:
                slot[offset] = p + 1
            else:
                named = neighbours_ref[p, number - (number > 13)]
                near_id = jnp.clip(named - s * blocks + 1, 0, slots)
                slot[offset] = jnp.where(named < 0, slots, near_id)

        for row in range(10):
            a, i = plane_of(row)

            def line(c):
                return jnp.concatenate(
                    [cubes[slot[a, -1, c], i, 7:8], cubes[slot[a, 0, c], i], cubes[slot[a, 1, c], i, 0:1]],
                    axis=0,
                )

            middle = line(0)
            views = (
                pltpu.roll(jnp.where(k == 7, line(-1), middle), 1, 1),
                middle,
                pltpu.roll(jnp.where(k == 0, line(1), middle), 7, 1),
            )
            for b in range(3):
                for c in range(3):
                    piece = views[c][b : b + 8].reshape(64, 128).astype(BF16)
                    patches[64 * row : 64 * row + 64, (3 * b + c) * 128 : (3 * b + c + 1) * 128] = piece

        product = lax.dot_general(
            weight_ref[...], patches[...], (((1,), (1,)), ((), ())), preferred_element_type=F32
        )
        pre_act = (
            product[:outs, 0:512] + product[outs : 2 * outs, 64:576] + product[2 * outs :, 128:640]
        )
        live = occupancy_ref[pl.ds(p, 1)].astype(F32)
        sigma = jax.nn.sigmoid(pre_act)
        act_ref[p] = (pre_act * sigma * live).astype(BF16)
        slope = sigma * (1.0 + pre_act * (1.0 - sigma))
        grad_pre = (cotangent_ref[p].astype(F32) * slope * live).astype(BF16)
        half = jnp.zeros((outs, 64), BF16)
        shifted[p, :outs, 0:512] = grad_pre
        shifted[p, outs : 2 * outs] = jnp.concatenate([half, grad_pre, half], axis=1)
        shifted[p, 2 * outs :, 128:640] = grad_pre
        wsum[...] += jnp.dot(shifted[p], patches[...], preferred_element_type=F32)
        return carry

    lax.fori_loop(0, blocks, forward, 0)

    for n in range(27):
        part = wsum[n // 9 * outs : (n // 9 + 1) * outs, n % 9 * 128 : (n % 9 + 1) * 128]
        wsend[outs * n : outs * (n + 1)] = part.astype(BF16)
    rest = wsend.shape[0] - 27 * outs
    if rest:
        wsend[27 * outs :] = jnp.zeros((rest, 128), BF16)
    height = ybuf.shape[1]

    def cut(parity, place):
        return pl.ds(pl.multiple_of((parity * 4 + place) * height, 16), height)

    def to_beside(j):
        place = lax.rem(z + 1 + j, 4)
        return copy(wsend.at[cut(1 - y, place)], ybuf.at[place], y_send, y_recv, j, (beside, c))

    def to_level(j):
        place = lax.rem(z + 1 + j, 4)
        return copy(zsend.at[j], zbuf.at[j], z_send, z_recv, j, (2 * place + y, c))

    if with_weight:
        for j in range(4):
            to_beside(j).start()

    def targets(rim):
        return [*range(1, blocks + 1), *([] if rim is None else [rim])]

    def backward(p, j, rim):
        grad_patches[...] = lax.dot_general(
            shifted[p], weight_ref[...], (((0,), (0,)), ((), ())), preferred_element_type=F32
        )
        share_of = {}
        for number, offset in offsets():
            if number == 13:
                named = s * blocks + p
            else:
                named = neighbours_ref[p, number - (number > 13)]
                named = jnp.where(named < 0, -9, named)
            for index, q in enumerate(targets(rim)):
                share_of[index, offset] = jnp.where(named == s * blocks - 1 + q, 1.0, 0.0).astype(F32)

        for row in range(10):
            a, i = plane_of(row)

            def part(b, c):
                column = (3 * b + c) * 128
                return grad_patches[64 * row : 64 * row + 64, column : column + 128].reshape(8, 8, 128)

            def line_sum(c):
                return (
                    jnp.concatenate([part(0, c), blank, blank], axis=0)
                    + jnp.concatenate([blank, part(1, c), blank], axis=0)
                    + jnp.concatenate([blank, blank, part(2, c)], axis=0)
                )

            below = pltpu.roll(line_sum(0), 7, 1)
            above = pltpu.roll(line_sum(2), 1, 1)
            zero = jnp.zeros_like(below)
            middle = line_sum(1) + jnp.where(k == 7, zero, below) + jnp.where(k == 0, zero, above)
            values = (jnp.where(k == 7, below, zero), middle, jnp.where(k == 0, above, zero))
            for index, q in enumerate(targets(rim)):

                def weighed(b, first, last):
                    return sum(share_of[index, (a, b, c - 1)] * values[c][first:last] for c in range(3))

                delta = weighed(0, 1, 9)
                delta = jnp.concatenate(
                    [delta[0:1] + weighed(1, 9, 10), delta[1:7], delta[7:8] + weighed(-1, 0, 1)], axis=0
                )
                sums[q, i] = sums[q, i] + delta

        if with_weight:
            to_beside(j).wait_recv()
            place = lax.rem(z + 1 + j, 4)
            joined = wsend[cut(y, place)].astype(F32) + ybuf[place].astype(F32)

            @pl.when(j < 3)
            def _():
                zsend[j] = joined.astype(BF16)
                to_level(j).start()

            @pl.when(j == 3)
            def _():
                wown[...] = joined

    kin, other = lax.div(c, 2), lax.div(far, 2)
    parts = (low, high, own)
    to_near = [
        copy(
            grads.at[which, lax.rem(near, 2) + 2 * h], near_buf.at[h, which],
            near_send, near_recv, 2 * index + h, (s, near),
        )
        for index, which in enumerate(parts)
        for h in range(2)
    ]
    to_far = [
        copy(passed.at[which], far_buf.at[which], far_send, far_recv, index, (s, far))
        for index, which in enumerate(parts)
    ]
    rims = [
        copy(rim_out.at[index], rim_in.at[index], rim_send, rim_recv, index, (peer, c))
        for index, peer in enumerate((before, after))
    ]
    sent = [
        rim_down, rim_up, own_near, high_far, low_far, high_near, low_near, high_pass, low_pass,
    ] + own_far + own_pass + to_near + to_far + rims

    def flip(slot):
        grads[slot] = sums[slot].reshape(512, 128).T.astype(BF16).reshape(4, share, 512)

    def merge_near(slot):
        passed[slot] = (grads[slot, far].astype(F32) + near_buf[other, slot].astype(F32)).astype(BF16)
        kept[slot] = grads[slot, c].astype(F32) + near_buf[kin, slot].astype(F32)

    def edges(t, carry):
        backward(t * (blocks - 1), t, t * (blocks + 1))
        return carry

    def inner(p, carry):
        @pl.when(p == blocks - 2)
        def _():
            for each in to_near[:4]:
                each.wait_recv()
            for index, slot in enumerate((low, high)):
                merge_near(slot)
                to_far[index].start()

        backward(p, p + 1, None)
        return carry

    lax.fori_loop(0, 2, edges, 0)
    flip(low)
    flip(high)
    for each in to_near[:4]:
        each.start()
    lax.fori_loop(1, blocks - 1, inner, 0)

    if with_weight:
        total = wown[...]
        for j in range(3):
            to_level(j).wait_recv()
            total = total + zbuf[j].astype(F32)
        wout_ref[cut(y, z)] = total.astype(BF16)
        mine = wout_ref.at[cut(y, z)]
        levels = [
            copy(mine, mine, zg_send, zg_recv, j, (2 * lax.rem(z + 1 + j, 4) + y, c)) for j in range(3)
        ]
        asides = []
        for j in range(4):
            piece = wout_ref.at[cut(y, lax.rem(z + 4 - j, 4))]
            asides.append(copy(piece, piece, yg_send, yg_recv, j, (beside, c)))
        for each in levels + asides[:1]:
            each.start()
        sent += levels + asides + [to_beside(j) for j in range(4)] + [to_level(j) for j in range(3)]
    else:
        wout_ref[...] = wsend[...]

    for slot in range(1, blocks + 1):
        flip(slot)
    for each in to_near[4:]:
        each.start()
    for index, slot in enumerate((low, high)):
        to_far[index].wait_recv()
        rim_out[index] = (kept[slot] + far_buf[slot].astype(F32)).astype(BF16)
        rims[index].start()
    for each in to_near[4:]:
        each.wait_recv()
    for slot in range(1, blocks + 1):
        merge_near(slot)
    to_far[2].start()
    if with_weight:
        for j in range(3):
            levels[j].wait_recv()
            asides[j + 1].start()
    to_far[2].wait_recv()
    for each in rims:
        each.wait_recv()
    for b in range(blocks):
        total = kept[1 + b] + far_buf[1 + b].astype(F32)
        if b == blocks - 1:
            total = total + rim_in[0].astype(F32)
        if b == 0:
            total = total + rim_in[1].astype(F32)
        out_ref[b] = (total * occupancy_ref[b : b + 1].astype(F32)).astype(BF16)
    if with_weight:
        for each in asides:
            each.wait_recv()
    for each in sent:
        each.wait_send()


def finish_kernel(
    scale, act_ref, grad_ref, wgrad_ref, act_out, grad_out, wgrad_out, taken, given, whole, load, save
):
    outs = wgrad_out.shape[1]
    height = 9 * outs
    copies = [
        pltpu.make_async_copy(act_ref, act_out, whole.at[0]),
        pltpu.make_async_copy(grad_ref, grad_out, whole.at[1]),
    ]
    loads = [
        pltpu.make_async_copy(wgrad_ref.at[pl.ds(height * i, height)], taken.at[i], load.at[i]) for i in range(3)
    ]
    saves = [
        pltpu.make_async_copy(given.at[pl.ds(9 * i, 9)], wgrad_out.at[pl.ds(9 * i, 9)], save.at[i]) for i in range(3)
    ]
    for each in loads + copies:
        each.start()
    for i in range(3):
        loads[i].wait()
        given[9 * i : 9 * i + 9] = taken[i].astype(F32).reshape(9, outs, 128) * scale
        saves[i].start()
    for each in copies + saves:
        each.wait()


def on_device(space_count, features, occupancy, weight, cotangent, neighbours):
    blocks, share = features.shape[:2]
    outs, _, cin = weight.shape
    slots = blocks + 2
    with_weight = space_count == 8 and blocks == 4
    height = -(-27 * outs // 128) * 16
    vmem = pl.BlockSpec(memory_space=pltpu.VMEM)
    hbm = pl.BlockSpec(memory_space=pltpu.HBM)
    dma = pltpu.SemaphoreType.DMA
    grid = (slots, share, 512)
    act, input_grad, wtotal = pl.pallas_call(
        functools.partial(whole_kernel, space_count, with_weight),
        out_shape=[
            jax.ShapeDtypeStruct(cotangent.shape, BF16),
            jax.ShapeDtypeStruct((blocks, share, 512), BF16),
            jax.ShapeDtypeStruct((8 * height, 128), BF16),
        ],
        in_specs=[hbm] * 5,
        out_specs=[vmem] * 3,
        scratch_shapes=[
            pltpu.SMEM(neighbours.shape, jnp.int32),
            pltpu.VMEM(features.shape, BF16),
            pltpu.VMEM(occupancy.shape, jnp.int32),
            pltpu.VMEM((3 * outs, 9 * cin), BF16),
            pltpu.VMEM(cotangent.shape, BF16),
            pltpu.VMEM((slots, 4, share, 512), BF16),
            pltpu.VMEM((slots + 1, 8, 8, 8, 128), F32),
            pltpu.VMEM((slots, 8, 8, 8, 128), F32),
            pltpu.VMEM((640, 9 * cin), BF16),
            pltpu.VMEM((640, 9 * cin), F32),
            pltpu.VMEM((blocks, 3 * outs, 640), BF16),
            pltpu.VMEM((3 * outs, 9 * cin), F32),
            pltpu.VMEM((8 * height, 128), BF16),
            pltpu.VMEM((4, height, 128), BF16),
            pltpu.VMEM((3, height, 128), BF16),
            pltpu.VMEM((3, height, 128), BF16),
            pltpu.VMEM((height, 128), F32),
            pltpu.VMEM((slots, 4, share, 512), BF16),
            pltpu.VMEM((2,) + grid, BF16),
            pltpu.VMEM(grid, F32),
            pltpu.VMEM(grid, BF16),
            pltpu.VMEM(grid, BF16),
            pltpu.VMEM((2, share, 512), BF16),
            pltpu.VMEM((2, share, 512), BF16),
        ]
        + [dma((n,)) for n in (31, 9 + 2 * blocks, 9 + 2 * blocks, 6, 6, 3, 3, 2, 2, 4, 4, 3, 3, 3, 3, 4, 4)],
        compiler_params=pltpu.CompilerParams(
            collective_id=0, has_side_effects=True, vmem_limit_bytes=63 * 2**20
        ),
        name="conv_both_ways",
    )(neighbours, features, occupancy, jnp.transpose(weight, (1, 0, 2)), cotangent)

    if not with_weight:
        wtotal = lax.psum(wtotal.astype(F32), "space")
    act, input_grad, weight_grad = pl.pallas_call(
        functools.partial(finish_kernel, (space_count * blocks * 512) ** -0.5),
        out_shape=[
            jax.ShapeDtypeStruct(act.shape, BF16),
            jax.ShapeDtypeStruct(input_grad.shape, BF16),
            jax.ShapeDtypeStruct((27, outs, cin), F32),
        ],
        in_specs=[hbm] * 3,
        out_specs=[hbm] * 3,
        scratch_shapes=[
            pltpu.VMEM((3, 9 * outs, cin), F32 if not with_weight else BF16),
            pltpu.VMEM((27, outs, cin), F32),
            dma((2,)), dma((3,)), dma((3,)),
        ],
        compiler_params=pltpu.CompilerParams(vmem_limit_bytes=63 * 2**20),
        name="finish",
    )(act, input_grad, wtotal)
    return (act, input_grad, jnp.transpose(weight_grad, (1, 0, 2)))


def solution(mesh):
    placed = (
        P("space", "chan", None),
        P("space", None),
        P("chan", None, None),
        P("space", "chan", None),
        P("space", None),
    )
    return jax.shard_map(
        functools.partial(on_device, mesh.shape["space"]),
        mesh=mesh,
        in_specs=placed,
        out_specs=(P("space", "chan", None), P("space", "chan", None), P("chan", None, None)),
        check_vma=False,
    )
```

```python
import functools

import jax
import jax.numpy as jnp
from jax import lax
from jax.experimental import pallas as pl
from jax.experimental.pallas import tpu as pltpu
from jax.sharding import PartitionSpec as P

MESH = pl.DeviceIdType.MESH
F32 = jnp.float32
BF16 = jnp.bfloat16


def places(space_count):
    s, c = lax.axis_index("space"), lax.axis_index("chan")
    before = lax.rem(s + space_count - 1, space_count)
    after = lax.rem(s + 1, space_count)
    near = c + 1 - 2 * lax.rem(c, 2)
    far = lax.rem(c + 2, 4)
    return s, c, before, after, near, far


def greet(peers):
    barrier = pltpu.get_barrier_semaphore()
    for peer in peers:
        pl.semaphore_signal(barrier, inc=1, device_id=peer, device_id_type=MESH)
    return lambda: pl.semaphore_wait(barrier, len(peers))


def whole_kernel(
    space_count, with_weight,
    neighbours_hbm, features_hbm, occupancy_hbm, weight_hbm, cotangent_hbm,
    act_ref, out_ref, wout_ref,
    neighbours_ref, features_ref, occupancy_ref, weight_ref, cotangent_ref, full, cubes, sums, patches, grad_patches, shifted, wsum,
    wsend, ybuf, zsend, zbuf, wown, grads, near_buf, kept, passed, far_buf, rim_out, rim_in,
    fetch, load_send, load_recv, near_send, near_recv, far_send, far_recv, rim_send, rim_recv,
    y_send, y_recv, z_send, z_recv, zg_send, zg_recv, yg_send, yg_recv,
):
    blocks, share = features_ref.shape[:2]
    outs = cotangent_ref.shape[1]
    slots = blocks + 2
    first = [
        pltpu.make_async_copy(occupancy_hbm, occupancy_ref, fetch.at[28]),
        pltpu.make_async_copy(features_hbm, features_ref, fetch.at[29]),
    ]
    fetches = [
        pltpu.make_async_copy(neighbours_hbm, neighbours_ref, fetch.at[30]),
        pltpu.make_async_copy(cotangent_hbm, cotangent_ref, fetch.at[27]),
    ]
    for n in range(27):
        rows, columns = pl.ds(n // 9 * outs, outs), pl.ds(n % 9 * 128, 128)
        fetches.append(pltpu.make_async_copy(weight_hbm.at[n], weight_ref.at[rows, columns], fetch.at[n]))
    for each in first + fetches:
        each.start()
    s, c, before, after, near, far = places(space_count)
    y = lax.rem(s, 2)
    z = lax.div(s, 2)
    beside = s + 1 - 2 * y

    def copy(source, target, send, recv, index, peer):
        return pltpu.make_async_remote_copy(
            src_ref=source,
            dst_ref=target,
            send_sem=send.at[index],
            recv_sem=recv.at[index],
            device_id=peer,
            device_id_type=MESH,
        )

    peers = [(before, c), (after, c), (s, near), (s, far)]
    if with_weight:
        peers += [(lax.rem(s + 2 * d, space_count), c) for d in range(1, 4)]
    greeted = greet(peers)

    def spread(slots_from, piece, slots_to, peer, index):
        return copy(full.at[slots_from, piece], full.at[slots_to, piece], load_send, load_recv, index, peer)

    own = pl.ds(1, blocks)
    low, high = 0, blocks + 1
    for each in first:
        each.wait()
    for b in (0, blocks - 1, *range(1, blocks - 1)):
        mask = occupancy_ref[b : b + 1].astype(F32)
        full[1 + b, c] = (features_ref[b].astype(F32) * mask).astype(BF16)
    rim_down = spread(1, c, high, (before, c), 0)
    rim_up = spread(blocks, c, low, (after, c), 1)
    own_near = spread(own, c, own, (s, near), 2)
    high_far = spread(high, c, high, (s, far), 3)
    low_far = spread(low, c, low, (s, far), 4)
    high_near = spread(high, c, high, (s, near), 5)
    low_near = spread(low, c, low, (s, near), 6)
    high_pass = spread(high, far, high, (s, near), 7)
    low_pass = spread(low, far, low, (s, near), 8)
    own_far = [spread(1 + b, c, 1 + b, (s, far), 9 + b) for b in range(blocks)]
    own_pass = [spread(1 + b, far, 1 + b, (s, near), 9 + blocks + b) for b in range(blocks)]
    greeted()
    for each in (rim_down, rim_up, *own_far, own_near):
        each.start()
    cubes[slots] = jnp.zeros((8, 8, 8, 128), F32)
    sums[...] = jnp.zeros(sums.shape, F32)
    wsum[...] = jnp.zeros(wsum.shape, F32)
    shifted[...] = jnp.zeros(shifted.shape, BF16)
    k = lax.broadcasted_iota(jnp.int32, (10, 8, 128), 1)
    blank = jnp.zeros((1, 8, 128), F32)
    for b in range(blocks):
        own_far[b].wait_recv()
        own_pass[b].start()
    rim_down.wait_recv()
    rim_up.wait_recv()
    for each in (high_far, low_far, high_near, low_near):
        each.start()

    def turn(slot):
        cubes[slot] = full[slot].reshape(4 * share, 512).astype(F32).T.reshape(8, 8, 8, 128)

    for each in fetches:
        each.wait()
    own_near.wait_recv()
    for b in range(blocks):
        own_pass[b].wait_recv()
        turn(1 + b)

    def plane_of(row):
        a = -1 if row == 0 else (1 if row == 9 else 0)
        return a, (row - 1) % 8

    def offsets():
        for number in range(27):
            yield number, (number // 9 - 1, number // 3 % 3 - 1, number % 3 - 1)

    def forward(t, carry):
        p = lax.rem(t + 1, blocks)

        @pl.when(t == blocks - 2)
        def _():
            high_far.wait_recv()
            low_far.wait_recv()
            high_pass.start()
            low_pass.start()
            for each in (high_near, low_near, high_pass, low_pass):
                each.wait_recv()
            turn(low)
            turn(high)

        slot = {}
        for number, offset in offsets():
            if number == 13:
                slot[offset] = p + 1
            else:
                named = neighbours_ref[p, number - (number > 13)]
                near_id = jnp.clip(named - s * blocks + 1, 0, slots)
                slot[offset] = jnp.where(named < 0, slots, near_id)

        for row in range(10):
            a, i = plane_of(row)

            def line(c):
                return jnp.concatenate(
                    [cubes[slot[a, -1, c], i, 7:8], cubes[slot[a, 0, c], i], cubes[slot[a, 1, c], i, 0:1]],
                    axis=0,
                )

            middle = line(0)
            views = (
                pltpu.roll(jnp.where(k == 7, line(-1), middle), 1, 1),
                middle,
                pltpu.roll(jnp.where(k == 0, line(1), middle), 7, 1),
            )
            for b in range(3):
                for c in range(3):
                    piece = views[c][b : b + 8].reshape(64, 128).astype(BF16)
                    patches[64 * row : 64 * row + 64, (3 * b + c) * 128 : (3 * b + c + 1) * 128] = piece

        product = lax.dot_general(
            weight_ref[...], patches[...], (((1,), (1,)), ((), ())), preferred_element_type=F32
        )
        pre_act = (
            product[:outs, 0:512] + product[outs : 2 * outs, 64:576] + product[2 * outs :, 128:640]
        )
        live = occupancy_ref[pl.ds(p, 1)].astype(F32)
        sigma = jax.nn.sigmoid(pre_act)
        act_ref[p] = (pre_act * sigma * live).astype(BF16)
        slope = sigma * (1.0 + pre_act * (1.0 - sigma))
        grad_pre = (cotangent_ref[p].astype(F32) * slope * live).astype(BF16)
        half = jnp.zeros((outs, 64), BF16)
        shifted[p, :outs, 0:512] = grad_pre
        shifted[p, outs : 2 * outs] = jnp.concatenate([half, grad_pre, half], axis=1)
        shifted[p, 2 * outs :, 128:640] = grad_pre
        wsum[...] += jnp.dot(shifted[p], patches[...], preferred_element_type=F32)
        return carry

    lax.fori_loop(0, blocks, forward, 0)

    for n in range(27):
        part = wsum[n // 9 * outs : (n // 9 + 1) * outs, n % 9 * 128 : (n % 9 + 1) * 128]
        wsend[outs * n : outs * (n + 1)] = part.astype(BF16)
    rest = wsend.shape[0] - 27 * outs
    if rest:
        wsend[27 * outs :] = jnp.zeros((rest, 128), BF16)
    height = ybuf.shape[1]

    def cut(parity, place):
        return pl.ds(pl.multiple_of((parity * 4 + place) * height, 16), height)

    def to_beside(j):
        place = lax.rem(z + 1 + j, 4)
        return copy(wsend.at[cut(1 - y, place)], ybuf.at[place], y_send, y_recv, j, (beside, c))

    def to_level(j):
        place = lax.rem(z + 1 + j, 4)
        return copy(zsend.at[j], zbuf.at[j], z_send, z_recv, j, (2 * place + y, c))

    if with_weight:
        for j in range(4):
            to_beside(j).start()

    def targets(rim):
        return [*range(1, blocks + 1), *([] if rim is None else [rim])]

    def backward(p, j, rim):
        grad_patches[...] = lax.dot_general(
            shifted[p], weight_ref[...], (((0,), (0,)), ((), ())), preferred_element_type=F32
        )
        share_of = {}
        for number, offset in offsets():
            if number == 13:
                named = s * blocks + p
            else:
                named = neighbours_ref[p, number - (number > 13)]
                named = jnp.where(named < 0, -9, named)
            for index, q in enumerate(targets(rim)):
                share_of[index, offset] = jnp.where(named == s * blocks - 1 + q, 1.0, 0.0).astype(F32)

        for row in range(10):
            a, i = plane_of(row)

            def part(b, c):
                column = (3 * b + c) * 128
                return grad_patches[64 * row : 64 * row + 64, column : column + 128].reshape(8, 8, 128)

            def line_sum(c):
                return (
                    jnp.concatenate([part(0, c), blank, blank], axis=0)
                    + jnp.concatenate([blank, part(1, c), blank], axis=0)
                    + jnp.concatenate([blank, blank, part(2, c)], axis=0)
                )

            below = pltpu.roll(line_sum(0), 7, 1)
            above = pltpu.roll(line_sum(2), 1, 1)
            zero = jnp.zeros_like(below)
            middle = line_sum(1) + jnp.where(k == 7, zero, below) + jnp.where(k == 0, zero, above)
            values = (jnp.where(k == 7, below, zero), middle, jnp.where(k == 0, above, zero))
            for index, q in enumerate(targets(rim)):

                def weighed(b, first, last):
                    return sum(share_of[index, (a, b, c - 1)] * values[c][first:last] for c in range(3))

                delta = weighed(0, 1, 9)
                delta = jnp.concatenate(
                    [delta[0:1] + weighed(1, 9, 10), delta[1:7], delta[7:8] + weighed(-1, 0, 1)], axis=0
                )
                sums[q, i] = sums[q, i] + delta

        if with_weight and rim is None:
            for step in range(2):
                chunk = 2 * (j - 2) + step
                to_beside(chunk).wait_recv()
                place = lax.rem(z + 1 + chunk, 4)
                joined = wsend[cut(y, place)].astype(F32) + ybuf[place].astype(F32)

                @pl.when(chunk < 3)
                def _():
                    zsend[chunk] = joined.astype(BF16)
                    to_level(chunk).start()

                @pl.when(chunk == 3)
                def _():
                    wown[...] = joined

    kin, other = lax.div(c, 2), lax.div(far, 2)
    parts = (low, high, own)
    to_near = [
        copy(
            grads.at[which, lax.rem(near, 2) + 2 * h], near_buf.at[h, which],
            near_send, near_recv, 2 * index + h, (s, near),
        )
        for index, which in enumerate(parts)
        for h in range(2)
    ]
    to_far = [
        copy(passed.at[which], far_buf.at[which], far_send, far_recv, index, (s, far))
        for index, which in enumerate(parts)
    ]
    rims = [
        copy(rim_out.at[index], rim_in.at[index], rim_send, rim_recv, index, (peer, c))
        for index, peer in enumerate((before, after))
    ]
    sent = [
        rim_down, rim_up, own_near, high_far, low_far, high_near, low_near, high_pass, low_pass,
    ] + own_far + own_pass + to_near + to_far + rims

    def flip(slot):
        grads[slot] = sums[slot].reshape(512, 128).T.astype(BF16).reshape(4, share, 512)

    def merge_near(slot):
        passed[slot] = (grads[slot, far].astype(F32) + near_buf[other, slot].astype(F32)).astype(BF16)
        kept[slot] = grads[slot, c].astype(F32) + near_buf[kin, slot].astype(F32)

    def edges(t, carry):
        backward(t * (blocks - 1), t, t * (blocks + 1))
        return carry

    def inner(p, carry):
        @pl.when(p == blocks - 2)
        def _():
            for each in to_near[:4]:
                each.wait_recv()
            for index, slot in enumerate((low, high)):
                merge_near(slot)
                to_far[index].start()

        backward(p, p + 1, None)
        return carry

    lax.fori_loop(0, 2, edges, 0)
    flip(low)
    flip(high)
    for each in to_near[:4]:
        each.start()
    lax.fori_loop(1, blocks - 1, inner, 0)

    for slot in range(1, blocks + 1):
        flip(slot)
    for each in to_near[4:]:
        each.start()
    if with_weight:
        total = wown[...]
        for j in range(3):
            to_level(j).wait_recv()
            total = total + zbuf[j].astype(F32)
        wout_ref[cut(y, z)] = total.astype(BF16)
        mine = wout_ref.at[cut(y, z)]
        levels = [
            copy(mine, mine, zg_send, zg_recv, j, (2 * lax.rem(z + 1 + j, 4) + y, c)) for j in range(3)
        ]
        asides = []
        for j in range(4):
            piece = wout_ref.at[cut(y, lax.rem(z + 4 - j, 4))]
            asides.append(copy(piece, piece, yg_send, yg_recv, j, (beside, c)))
        for each in levels + asides[:1]:
            each.start()
        sent += levels + asides + [to_beside(j) for j in range(4)] + [to_level(j) for j in range(3)]
    else:
        wout_ref[...] = wsend[...]

    for index, slot in enumerate((low, high)):
        to_far[index].wait_recv()
        rim_out[index] = (kept[slot] + far_buf[slot].astype(F32)).astype(BF16)
        rims[index].start()
    for each in to_near[4:]:
        each.wait_recv()
    for slot in range(1, blocks + 1):
        merge_near(slot)
    to_far[2].start()
    if with_weight:
        for j in range(3):
            levels[j].wait_recv()
            asides[j + 1].start()
    to_far[2].wait_recv()
    for each in rims:
        each.wait_recv()
    for b in range(blocks):
        total = kept[1 + b] + far_buf[1 + b].astype(F32)
        if b == blocks - 1:
            total = total + rim_in[0].astype(F32)
        if b == 0:
            total = total + rim_in[1].astype(F32)
        out_ref[b] = (total * occupancy_ref[b : b + 1].astype(F32)).astype(BF16)
    if with_weight:
        for each in asides:
            each.wait_recv()
    for each in sent:
        each.wait_send()


def finish_kernel(
    scale, act_ref, grad_ref, wgrad_ref, act_out, grad_out, wgrad_out,
    act_buf, grad_buf, taken, given, load, save,
):
    outs = wgrad_out.shape[1]
    height = 9 * outs
    loads = [
        pltpu.make_async_copy(wgrad_ref.at[pl.ds(height * i, height)], taken.at[i], load.at[i]) for i in range(3)
    ]
    saves = [
        pltpu.make_async_copy(given.at[pl.ds(9 * i, 9)], wgrad_out.at[pl.ds(9 * i, 9)], save.at[i]) for i in range(3)
    ]
    for i, (source, held, target) in enumerate(((act_ref, act_buf, act_out), (grad_ref, grad_buf, grad_out))):
        loads.append(pltpu.make_async_copy(source, held, load.at[3 + i]))
        saves.append(pltpu.make_async_copy(held, target, save.at[3 + i]))
    for each in loads:
        each.start()
    for i in range(5):
        loads[i].wait()
        if i < 3:
            given[9 * i : 9 * i + 9] = taken[i].astype(F32).reshape(9, outs, 128) * scale
        saves[i].start()
    for each in saves:
        each.wait()


def on_device(space_count, features, occupancy, weight, cotangent, neighbours):
    blocks, share = features.shape[:2]
    outs, _, cin = weight.shape
    slots = blocks + 2
    with_weight = space_count == 8 and blocks == 4
    height = -(-27 * outs // 128) * 16
    vmem = pl.BlockSpec(memory_space=pltpu.VMEM)
    hbm = pl.BlockSpec(memory_space=pltpu.HBM)
    dma = pltpu.SemaphoreType.DMA
    grid = (slots, share, 512)
    act, input_grad, wtotal = pl.pallas_call(
        functools.partial(whole_kernel, space_count, with_weight),
        out_shape=[
            jax.ShapeDtypeStruct(cotangent.shape, BF16),
            jax.ShapeDtypeStruct((blocks, share, 512), BF16),
            jax.ShapeDtypeStruct((8 * height, 128), BF16),
        ],
        in_specs=[hbm] * 5,
        out_specs=[vmem] * 3,
        scratch_shapes=[
            pltpu.SMEM(neighbours.shape, jnp.int32),
            pltpu.VMEM(features.shape, BF16),
            pltpu.VMEM(occupancy.shape, jnp.int32),
            pltpu.VMEM((3 * outs, 9 * cin), BF16),
            pltpu.VMEM(cotangent.shape, BF16),
            pltpu.VMEM((slots, 4, share, 512), BF16),
            pltpu.VMEM((slots + 1, 8, 8, 8, 128), F32),
            pltpu.VMEM((slots, 8, 8, 8, 128), F32),
            pltpu.VMEM((640, 9 * cin), BF16),
            pltpu.VMEM((640, 9 * cin), F32),
            pltpu.VMEM((blocks, 3 * outs, 640), BF16),
            pltpu.VMEM((3 * outs, 9 * cin), F32),
            pltpu.VMEM((8 * height, 128), BF16),
            pltpu.VMEM((4, height, 128), BF16),
            pltpu.VMEM((3, height, 128), BF16),
            pltpu.VMEM((3, height, 128), BF16),
            pltpu.VMEM((height, 128), F32),
            pltpu.VMEM((slots, 4, share, 512), BF16),
            pltpu.VMEM((2,) + grid, BF16),
            pltpu.VMEM(grid, F32),
            pltpu.VMEM(grid, BF16),
            pltpu.VMEM(grid, BF16),
            pltpu.VMEM((2, share, 512), BF16),
            pltpu.VMEM((2, share, 512), BF16),
        ]
        + [dma((n,)) for n in (31, 9 + 2 * blocks, 9 + 2 * blocks, 6, 6, 3, 3, 2, 2, 4, 4, 3, 3, 3, 3, 4, 4)],
        compiler_params=pltpu.CompilerParams(
            collective_id=0, has_side_effects=True, vmem_limit_bytes=63 * 2**20
        ),
        name="conv_both_ways",
    )(neighbours, features, occupancy, jnp.transpose(weight, (1, 0, 2)), cotangent)

    if not with_weight:
        wtotal = lax.psum(wtotal.astype(F32), "space")
    act, input_grad, weight_grad = pl.pallas_call(
        functools.partial(finish_kernel, (space_count * blocks * 512) ** -0.5),
        out_shape=[
            jax.ShapeDtypeStruct(act.shape, BF16),
            jax.ShapeDtypeStruct(input_grad.shape, BF16),
            jax.ShapeDtypeStruct((27, outs, cin), F32),
        ],
        in_specs=[hbm] * 3,
        out_specs=[hbm] * 3,
        scratch_shapes=[
            pltpu.VMEM(act.shape, BF16),
            pltpu.VMEM(input_grad.shape, BF16),
            pltpu.VMEM((3, 9 * outs, cin), F32 if not with_weight else BF16),
            pltpu.VMEM((27, outs, cin), F32),
            dma((5,)), dma((5,)),
        ],
        compiler_params=pltpu.CompilerParams(vmem_limit_bytes=63 * 2**20),
        name="finish",
    )(act, input_grad, wtotal)
    return (act, input_grad, jnp.transpose(weight_grad, (1, 0, 2)))


def solution(mesh):
    placed = (
        P("space", "chan", None),
        P("space", None),
        P("chan", None, None),
        P("space", "chan", None),
        P("space", None),
    )
    return jax.shard_map(
        functools.partial(on_device, mesh.shape["space"]),
        mesh=mesh,
        in_specs=placed,
        out_specs=(P("space", "chan", None), P("space", "chan", None), P("chan", None, None)),
        check_vma=False,
    )
```

```python
import functools

import jax
import jax.numpy as jnp
from jax import lax
from jax.experimental import pallas as pl
from jax.experimental.pallas import tpu as pltpu
from jax.sharding import PartitionSpec as P

MESH = pl.DeviceIdType.MESH
F32 = jnp.float32
BF16 = jnp.bfloat16


def places(space_count):
    s, c = lax.axis_index("space"), lax.axis_index("chan")
    before = lax.rem(s + space_count - 1, space_count)
    after = lax.rem(s + 1, space_count)
    near = c + 1 - 2 * lax.rem(c, 2)
    far = lax.rem(c + 2, 4)
    return s, c, before, after, near, far


def greet(peers):
    barrier = pltpu.get_barrier_semaphore()
    for peer in peers:
        pl.semaphore_signal(barrier, inc=1, device_id=peer, device_id_type=MESH)
    return lambda: pl.semaphore_wait(barrier, len(peers))


def whole_kernel(
    space_count, with_weight,
    neighbours_hbm, features_hbm, occupancy_hbm, weight_hbm, cotangent_hbm,
    act_ref, out_ref, wout_ref,
    neighbours_ref, features_ref, occupancy_ref, weight_ref, cotangent_ref, full, cubes, sums, patches, grad_patches, shifted, wsum,
    wsend, ybuf, zsend, zbuf, wown, grads, near_buf, kept, passed, far_buf, rim_out, rim_in,
    fetch, load_send, load_recv, near_send, near_recv, far_send, far_recv, rim_send, rim_recv,
    y_send, y_recv, z_send, z_recv, zg_send, zg_recv, yg_send, yg_recv,
):
    blocks, share = features_ref.shape[:2]
    outs = cotangent_ref.shape[1]
    slots = blocks + 2
    first = [
        pltpu.make_async_copy(occupancy_hbm, occupancy_ref, fetch.at[28]),
        pltpu.make_async_copy(features_hbm, features_ref, fetch.at[29]),
    ]
    fetches = [
        pltpu.make_async_copy(neighbours_hbm, neighbours_ref, fetch.at[30]),
        pltpu.make_async_copy(cotangent_hbm, cotangent_ref, fetch.at[27]),
    ]
    for n in range(27):
        rows, columns = pl.ds(n // 9 * outs, outs), pl.ds(n % 9 * 128, 128)
        fetches.append(pltpu.make_async_copy(weight_hbm.at[n], weight_ref.at[rows, columns], fetch.at[n]))
    for each in first + fetches:
        each.start()
    s, c, before, after, near, far = places(space_count)
    y = lax.rem(s, 2)
    z = lax.div(s, 2)
    beside = s + 1 - 2 * y

    def copy(source, target, send, recv, index, peer):
        return pltpu.make_async_remote_copy(
            src_ref=source,
            dst_ref=target,
            send_sem=send.at[index],
            recv_sem=recv.at[index],
            device_id=peer,
            device_id_type=MESH,
        )

    peers = [(before, c), (after, c), (s, near), (s, far)]
    if with_weight:
        peers += [(lax.rem(s + 2 * d, space_count), c) for d in range(1, 4)]
    greeted = greet(peers)

    def spread(slots_from, piece, slots_to, peer, index):
        return copy(full.at[slots_from, piece], full.at[slots_to, piece], load_send, load_recv, index, peer)

    own = pl.ds(1, blocks)
    low, high = 0, blocks + 1
    for each in first:
        each.wait()
    for b in (0, blocks - 1, *range(1, blocks - 1)):
        mask = occupancy_ref[b : b + 1].astype(F32)
        full[1 + b, c] = (features_ref[b].astype(F32) * mask).astype(BF16)
    rim_down = spread(1, c, high, (before, c), 0)
    rim_up = spread(blocks, c, low, (after, c), 1)
    own_far = spread(own, c, own, (s, far), 2)
    own_near = spread(own, c, own, (s, near), 3)
    high_far = spread(high, c, high, (s, far), 4)
    low_far = spread(low, c, low, (s, far), 5)
    high_near = spread(high, c, high, (s, near), 6)
    low_near = spread(low, c, low, (s, near), 7)
    own_pass = spread(own, far, own, (s, near), 8)
    high_pass = spread(high, far, high, (s, near), 9)
    low_pass = spread(low, far, low, (s, near), 10)
    greeted()
    for each in (rim_down, rim_up, own_far, own_near):
        each.start()
    cubes[slots] = jnp.zeros((8, 8, 8, 128), F32)
    sums[...] = jnp.zeros(sums.shape, F32)
    wsum[...] = jnp.zeros(wsum.shape, F32)
    shifted[...] = jnp.zeros(shifted.shape, BF16)
    k = lax.broadcasted_iota(jnp.int32, (10, 8, 128), 1)
    blank = jnp.zeros((1, 8, 128), F32)
    own_far.wait_recv()
    own_pass.start()
    rim_down.wait_recv()
    rim_up.wait_recv()
    for each in (high_far, low_far, high_near, low_near):
        each.start()

    def turn(slot):
        cubes[slot] = full[slot].reshape(4 * share, 512).astype(F32).T.reshape(8, 8, 8, 128)

    for each in fetches:
        each.wait()
    own_near.wait_recv()
    own_pass.wait_recv()
    for slot in range(1, blocks + 1):
        turn(slot)

    def plane_of(row):
        a = -1 if row == 0 else (1 if row == 9 else 0)
        return a, (row - 1) % 8

    def offsets():
        for number in range(27):
            yield number, (number // 9 - 1, number // 3 % 3 - 1, number % 3 - 1)

    def build(t):
        p = (t + 1) % blocks
        if t == blocks - 2:
            high_far.wait_recv()
            low_far.wait_recv()
            high_pass.start()
            low_pass.start()
            for each in (high_near, low_near, high_pass, low_pass):
                each.wait_recv()
            turn(low)
            turn(high)

        slot = {}
        for number, offset in offsets():
            if number == 13:
                slot[offset] = p + 1
            else:
                named = neighbours_ref[p, number - (number > 13)]
                near_id = jnp.clip(named - s * blocks + 1, 0, slots)
                slot[offset] = jnp.where(named < 0, slots, near_id)

        for row in range(10):
            a, i = plane_of(row)

            def line(c):
                return jnp.concatenate(
                    [cubes[slot[a, -1, c], i, 7:8], cubes[slot[a, 0, c], i], cubes[slot[a, 1, c], i, 0:1]],
                    axis=0,
                )

            middle = line(0)
            views = (
                pltpu.roll(jnp.where(k == 7, line(-1), middle), 1, 1),
                middle,
                pltpu.roll(jnp.where(k == 0, line(1), middle), 7, 1),
            )
            for b in range(3):
                for c in range(3):
                    piece = views[c][b : b + 8].reshape(64, 128).astype(BF16)
                    patches[t % 2, 64 * row : 64 * row + 64, (3 * b + c) * 128 : (3 * b + c + 1) * 128] = piece

    def forward(t):
        p = (t + 1) % blocks
        product = lax.dot_general(
            weight_ref[...], patches[t % 2], (((1,), (1,)), ((), ())), preferred_element_type=F32
        )
        if t + 1 < blocks:
            build(t + 1)
        pre_act = (
            product[:outs, 0:512] + product[outs : 2 * outs, 64:576] + product[2 * outs :, 128:640]
        )
        live = occupancy_ref[p : p + 1].astype(F32)
        sigma = jax.nn.sigmoid(pre_act)
        act_ref[p] = (pre_act * sigma * live).astype(BF16)
        slope = sigma * (1.0 + pre_act * (1.0 - sigma))
        grad_pre = (cotangent_ref[p].astype(F32) * slope * live).astype(BF16)
        half = jnp.zeros((outs, 64), BF16)
        shifted[p, :outs, 0:512] = grad_pre
        shifted[p, outs : 2 * outs] = jnp.concatenate([half, grad_pre, half], axis=1)
        shifted[p, 2 * outs :, 128:640] = grad_pre
        wsum[...] += jnp.dot(shifted[p], patches[t % 2], preferred_element_type=F32)

    build(0)
    for t in range(blocks):
        forward(t)

    for n in range(27):
        part = wsum[n // 9 * outs : (n // 9 + 1) * outs, n % 9 * 128 : (n % 9 + 1) * 128]
        wsend[outs * n : outs * (n + 1)] = part.astype(BF16)
    rest = wsend.shape[0] - 27 * outs
    if rest:
        wsend[27 * outs :] = jnp.zeros((rest, 128), BF16)
    height = ybuf.shape[1]

    def cut(parity, place):
        return pl.ds(pl.multiple_of((parity * 4 + place) * height, 16), height)

    def to_beside(j):
        place = lax.rem(z + 1 + j, 4)
        return copy(wsend.at[cut(1 - y, place)], ybuf.at[place], y_send, y_recv, j, (beside, c))

    def to_level(j):
        place = lax.rem(z + 1 + j, 4)
        return copy(zsend.at[j], zbuf.at[j], z_send, z_recv, j, (2 * place + y, c))

    if with_weight:
        for j in range(4):
            to_beside(j).start()

    def targets(rim):
        return [*range(1, blocks + 1), *([] if rim is None else [rim])]

    def backward(p, j, rim):
        grad_patches[...] = lax.dot_general(
            shifted[p], weight_ref[...], (((0,), (0,)), ((), ())), preferred_element_type=F32
        )
        share_of = {}
        for number, offset in offsets():
            if number == 13:
                named = s * blocks + p
            else:
                named = neighbours_ref[p, number - (number > 13)]
                named = jnp.where(named < 0, -9, named)
            for index, q in enumerate(targets(rim)):
                share_of[index, offset] = jnp.where(named == s * blocks - 1 + q, 1.0, 0.0).astype(F32)

        for row in range(10):
            a, i = plane_of(row)

            def part(b, c):
                column = (3 * b + c) * 128
                return grad_patches[64 * row : 64 * row + 64, column : column + 128].reshape(8, 8, 128)

            def line_sum(c):
                return (
                    jnp.concatenate([part(0, c), blank, blank], axis=0)
                    + jnp.concatenate([blank, part(1, c), blank], axis=0)
                    + jnp.concatenate([blank, blank, part(2, c)], axis=0)
                )

            below = pltpu.roll(line_sum(0), 7, 1)
            above = pltpu.roll(line_sum(2), 1, 1)
            zero = jnp.zeros_like(below)
            middle = line_sum(1) + jnp.where(k == 7, zero, below) + jnp.where(k == 0, zero, above)
            values = (jnp.where(k == 7, below, zero), middle, jnp.where(k == 0, above, zero))
            for index, q in enumerate(targets(rim)):

                def weighed(b, first, last):
                    return sum(share_of[index, (a, b, c - 1)] * values[c][first:last] for c in range(3))

                delta = weighed(0, 1, 9)
                delta = jnp.concatenate(
                    [delta[0:1] + weighed(1, 9, 10), delta[1:7], delta[7:8] + weighed(-1, 0, 1)], axis=0
                )
                sums[q, i] = sums[q, i] + delta

        if with_weight:
            to_beside(j).wait_recv()
            place = lax.rem(z + 1 + j, 4)
            joined = wsend[cut(y, place)].astype(F32) + ybuf[place].astype(F32)

            @pl.when(j < 3)
            def _():
                zsend[j] = joined.astype(BF16)
                to_level(j).start()

            @pl.when(j == 3)
            def _():
                wown[...] = joined

    kin, other = lax.div(c, 2), lax.div(far, 2)
    parts = (low, high, own)
    to_near = [
        copy(
            grads.at[which, lax.rem(near, 2) + 2 * h], near_buf.at[h, which],
            near_send, near_recv, 2 * index + h, (s, near),
        )
        for index, which in enumerate(parts)
        for h in range(2)
    ]
    to_far = [
        copy(passed.at[which], far_buf.at[which], far_send, far_recv, index, (s, far))
        for index, which in enumerate(parts)
    ]
    rims = [
        copy(rim_out.at[index], rim_in.at[index], rim_send, rim_recv, index, (peer, c))
        for index, peer in enumerate((before, after))
    ]
    sent = [
        rim_down, rim_up, own_far, own_near, high_far, low_far,
        high_near, low_near, own_pass, high_pass, low_pass,
    ] + to_near + to_far + rims

    def flip(slot):
        grads[slot] = sums[slot].reshape(512, 128).T.astype(BF16).reshape(4, share, 512)

    def merge_near(slot):
        passed[slot] = (grads[slot, far].astype(F32) + near_buf[other, slot].astype(F32)).astype(BF16)
        kept[slot] = grads[slot, c].astype(F32) + near_buf[kin, slot].astype(F32)

    def edges(t, carry):
        backward(t * (blocks - 1), t, t * (blocks + 1))
        return carry

    def inner(p, carry):
        @pl.when(p == blocks - 2)
        def _():
            for each in to_near[:4]:
                each.wait_recv()
            for index, slot in enumerate((low, high)):
                merge_near(slot)
                to_far[index].start()

        backward(p, p + 1, None)
        return carry

    lax.fori_loop(0, 2, edges, 0)
    flip(low)
    flip(high)
    for each in to_near[:4]:
        each.start()
    lax.fori_loop(1, blocks - 1, inner, 0)

    for slot in range(1, blocks + 1):
        flip(slot)
    for each in to_near[4:]:
        each.start()
    if with_weight:
        total = wown[...]
        for j in range(3):
            to_level(j).wait_recv()
            total = total + zbuf[j].astype(F32)
        wout_ref[cut(y, z)] = total.astype(BF16)
        mine = wout_ref.at[cut(y, z)]
        levels = [
            copy(mine, mine, zg_send, zg_recv, j, (2 * lax.rem(z + 1 + j, 4) + y, c)) for j in range(3)
        ]
        asides = []
        for j in range(4):
            piece = wout_ref.at[cut(y, lax.rem(z + 4 - j, 4))]
            asides.append(copy(piece, piece, yg_send, yg_recv, j, (beside, c)))
        for each in levels + asides[:1]:
            each.start()
        sent += levels + asides + [to_beside(j) for j in range(4)] + [to_level(j) for j in range(3)]
    else:
        wout_ref[...] = wsend[...]

    for index, slot in enumerate((low, high)):
        to_far[index].wait_recv()
        rim_out[index] = (kept[slot] + far_buf[slot].astype(F32)).astype(BF16)
        rims[index].start()
    for each in to_near[4:]:
        each.wait_recv()
    for slot in range(1, blocks + 1):
        merge_near(slot)
    to_far[2].start()
    if with_weight:
        for j in range(3):
            levels[j].wait_recv()
            asides[j + 1].start()
    to_far[2].wait_recv()
    for each in rims:
        each.wait_recv()
    for b in range(blocks):
        total = kept[1 + b] + far_buf[1 + b].astype(F32)
        if b == blocks - 1:
            total = total + rim_in[0].astype(F32)
        if b == 0:
            total = total + rim_in[1].astype(F32)
        out_ref[b] = (total * occupancy_ref[b : b + 1].astype(F32)).astype(BF16)
    if with_weight:
        for each in asides:
            each.wait_recv()
    for each in sent:
        each.wait_send()


def finish_kernel(
    scale, act_ref, grad_ref, wgrad_ref, act_out, grad_out, wgrad_out,
    act_buf, grad_buf, taken, given, load, save,
):
    outs = wgrad_out.shape[1]
    height = 9 * outs
    loads = [
        pltpu.make_async_copy(wgrad_ref.at[pl.ds(height * i, height)], taken.at[i], load.at[i]) for i in range(3)
    ]
    saves = [
        pltpu.make_async_copy(given.at[pl.ds(9 * i, 9)], wgrad_out.at[pl.ds(9 * i, 9)], save.at[i]) for i in range(3)
    ]
    for i, (source, held, target) in enumerate(((act_ref, act_buf, act_out), (grad_ref, grad_buf, grad_out))):
        loads.append(pltpu.make_async_copy(source, held, load.at[3 + i]))
        saves.append(pltpu.make_async_copy(held, target, save.at[3 + i]))
    for each in loads:
        each.start()
    for i in range(5):
        loads[i].wait()
        if i < 3:
            given[9 * i : 9 * i + 9] = taken[i].astype(F32).reshape(9, outs, 128) * scale
        saves[i].start()
    for each in saves:
        each.wait()


def on_device(space_count, features, occupancy, weight, cotangent, neighbours):
    blocks, share = features.shape[:2]
    outs, _, cin = weight.shape
    slots = blocks + 2
    with_weight = space_count == 8 and blocks == 4
    height = -(-27 * outs // 128) * 16
    vmem = pl.BlockSpec(memory_space=pltpu.VMEM)
    hbm = pl.BlockSpec(memory_space=pltpu.HBM)
    dma = pltpu.SemaphoreType.DMA
    grid = (slots, share, 512)
    act, input_grad, wtotal = pl.pallas_call(
        functools.partial(whole_kernel, space_count, with_weight),
        out_shape=[
            jax.ShapeDtypeStruct(cotangent.shape, BF16),
            jax.ShapeDtypeStruct((blocks, share, 512), BF16),
            jax.ShapeDtypeStruct((8 * height, 128), BF16),
        ],
        in_specs=[hbm] * 5,
        out_specs=[vmem] * 3,
        scratch_shapes=[
            pltpu.SMEM(neighbours.shape, jnp.int32),
            pltpu.VMEM(features.shape, BF16),
            pltpu.VMEM(occupancy.shape, jnp.int32),
            pltpu.VMEM((3 * outs, 9 * cin), BF16),
            pltpu.VMEM(cotangent.shape, BF16),
            pltpu.VMEM((slots, 4, share, 512), BF16),
            pltpu.VMEM((slots + 1, 8, 8, 8, 128), F32),
            pltpu.VMEM((slots, 8, 8, 8, 128), F32),
            pltpu.VMEM((2, 640, 9 * cin), BF16),
            pltpu.VMEM((640, 9 * cin), F32),
            pltpu.VMEM((blocks, 3 * outs, 640), BF16),
            pltpu.VMEM((3 * outs, 9 * cin), F32),
            pltpu.VMEM((8 * height, 128), BF16),
            pltpu.VMEM((4, height, 128), BF16),
            pltpu.VMEM((3, height, 128), BF16),
            pltpu.VMEM((3, height, 128), BF16),
            pltpu.VMEM((height, 128), F32),
            pltpu.VMEM((slots, 4, share, 512), BF16),
            pltpu.VMEM((2,) + grid, BF16),
            pltpu.VMEM(grid, F32),
            pltpu.VMEM(grid, BF16),
            pltpu.VMEM(grid, BF16),
            pltpu.VMEM((2, share, 512), BF16),
            pltpu.VMEM((2, share, 512), BF16),
        ]
        + [dma((n,)) for n in (31, 11, 11, 6, 6, 3, 3, 2, 2, 4, 4, 3, 3, 3, 3, 4, 4)],
        compiler_params=pltpu.CompilerParams(
            collective_id=0, has_side_effects=True, vmem_limit_bytes=63 * 2**20
        ),
        name="conv_both_ways",
    )(neighbours, features, occupancy, jnp.transpose(weight, (1, 0, 2)), cotangent)

    if not with_weight:
        wtotal = lax.psum(wtotal.astype(F32), "space")
    act, input_grad, weight_grad = pl.pallas_call(
        functools.partial(finish_kernel, (space_count * blocks * 512) ** -0.5),
        out_shape=[
            jax.ShapeDtypeStruct(act.shape, BF16),
            jax.ShapeDtypeStruct(input_grad.shape, BF16),
            jax.ShapeDtypeStruct((27, outs, cin), F32),
        ],
        in_specs=[hbm] * 3,
        out_specs=[hbm] * 3,
        scratch_shapes=[
            pltpu.VMEM(act.shape, BF16),
            pltpu.VMEM(input_grad.shape, BF16),
            pltpu.VMEM((3, 9 * outs, cin), F32 if not with_weight else BF16),
            pltpu.VMEM((27, outs, cin), F32),
            dma((5,)), dma((5,)),
        ],
        compiler_params=pltpu.CompilerParams(vmem_limit_bytes=63 * 2**20),
        name="finish",
    )(act, input_grad, wtotal)
    return (act, input_grad, jnp.transpose(weight_grad, (1, 0, 2)))


def solution(mesh):
    placed = (
        P("space", "chan", None),
        P("space", None),
        P("chan", None, None),
        P("space", "chan", None),
        P("space", None),
    )
    return jax.shard_map(
        functools.partial(on_device, mesh.shape["space"]),
        mesh=mesh,
        in_specs=placed,
        out_specs=(P("space", "chan", None), P("space", "chan", None), P("chan", None, None)),
        check_vma=False,
    )
```
